32 devices in a mesh: fsdp: 32 (over z, y, x, core), tp: 1.
Axes of the slice: x: 2, y: 2, z: 4, core: 2. Of those that a mesh axis runs over, the one named last changes fastest.
Arguments:
- momentum: float32 [32, 26624], P('fsdp', 'tp'), may hold values from -510 to 510
- gradient: float32 [32, 26624], P('fsdp', 'tp'), may hold values from -6 to 6
- basis: float32 [2, 26624], P(None, 'tp'), may hold values from -0.0390625 to 0.0390625
- weight: bfloat16 [32, 26624], P('fsdp', 'tp'), may hold values from -1 to 1
- inputs: bfloat16 [4096, 32], P('fsdp'), may hold values from -6 to 6
Outputs:
- new_momentum: float32 [32, 26624], P('fsdp', 'tp')
- new_basis: float32 [2, 26624], P(None, 'tp')
- new_weight: bfloat16 [32, 26624], P('fsdp', 'tp')
- activations: bfloat16 [4096, 26624], P('fsdp', 'tp')
The draws below stay inside these ranges and needn't reach their ends.
All inputs are finite; a program needn't handle non-finite values.
Results may differ from the reference program's by a relative error of at most 0.0049.
Values may be sent and summed in bfloat16 or wider, within the bound.
A program may use at most 64 MiB of HBM per device.

```python
import math
import jax
import jax.numpy as jnp
from jax import lax

N = 26624
TOK_DEV = 128
ROWS = 32
RANK = 2
TOKENS = 4096


def draw_momentum(key, part):
    keys = jax.random.split(key, 3)
    row_ids = jnp.arange(ROWS, dtype=jnp.float32)
    col_ids = jnp.arange(N, dtype=jnp.float32)
    rough_rows = jnp.exp(jax.random.uniform(keys[0], (ROWS,), minval=-0.69, maxval=0.69))
    rough_cols = jnp.exp(jax.random.uniform(keys[1], (N,), minval=-0.69, maxval=0.69))
    base = jnp.clip(jax.random.normal(keys[2], (ROWS, N)), -5.0, 5.0)
    rise = 3.0
    ramp_rows = jnp.exp(math.log(rise) * row_ids / (ROWS - 1))
    ramp_cols = jnp.exp(math.log(rise) * col_ids / (N - 1))
    values = base * (rough_rows * ramp_rows)[:, None] * (rough_cols * ramp_cols)[None, :]
    return jnp.clip(values, -510.0, 510.0).astype(jnp.float32)


def spiked(result, rng, source, target, blocks, factor):
    owner, partner = [(jnp.arange(result.shape[dim]) // (result.shape[dim] // blocks)).reshape([-1 if axis == dim else 1 for axis in range(result.ndim)]) for dim in (source, target)]
    chosen = jax.random.permutation(rng, blocks)[partner]
    strong = (owner == chosen) | (owner == (partner + blocks // 2) % blocks)
    return jnp.where(strong, factor * result, result)


def level_of(rng, shape, shards, smallest, top_value):
    def one(dim, blocks):
        draws = jax.random.uniform(jax.random.fold_in(jax.random.fold_in(rng, 6), dim), (blocks,), jnp.float32, smallest / len(shards), top_value / len(shards))
        return jnp.repeat(jnp.exp(draws), shape[dim] // blocks).reshape((-1,) + (1,) * (len(shape) - dim - 1))

    level = one(*shards[0])
    for cut in shards[1:]:
        level = level * one(*cut)
    return level


def bell_draw(stream_key, shape, width, bound, cuts=(), kind=jnp.bfloat16):
    drawn = jax.random.normal(stream_key, shape, jnp.float32) * width
    if len(cuts) > 0:
        drawn = level_of(stream_key, shape, cuts, -0.22, 0.18) * drawn
    return jnp.clip(drawn, min=-bound, max=bound).astype(kind)


def heavy_noise(rng, dims, width, reach, cuts, heavy, held_as=jnp.bfloat16):
    drawn = width * jax.random.normal(rng, dims, jnp.float32)
    if cuts:
        drawn = drawn * level_of(rng, dims, cuts, -0.22, 0.18)
    return jnp.clip(spiked(drawn, jax.random.fold_in(rng, 3), *heavy), -reach, reach).astype(held_as)


def setup_inputs(seed: int = 0) -> dict:
    seeds = jax.random.split(jax.random.key(seed), 6)
    momentum = draw_momentum(jax.random.fold_in(seeds[5], 71), 0)
    gradient = heavy_noise(seeds[1], (ROWS, N), 1.0, 6.0, ((0, 32),), (0, 1, 32, 2.75), jnp.float32)
    basis = bell_draw(seeds[2], (RANK, N), N ** -0.5, 0.0390625, (), jnp.float32)
    weight = bell_draw(seeds[3], (ROWS, N), ROWS ** -0.5, 1.0, ((0, 32),))
    inputs = bell_draw(seeds[4], (TOKENS, ROWS), 1.0, 6.0, ((0, 32),))
    return dict(momentum=momentum, gradient=gradient, basis=basis, weight=weight, inputs=inputs)


decay_rate = 0.8
step_size = 0.5
epsilon = 1e-06
highest = lax.Precision.HIGHEST

def product(left, right):
    return jnp.dot(left.astype(jnp.float32), right.astype(jnp.float32), precision=highest, preferred_element_type=jnp.float32)

def reference(momentum, gradient, basis, weight, inputs):
    buffer = decay_rate * momentum + gradient
    power = product(buffer, basis.T)
    gram = product(power.T, power)
    lower = jnp.linalg.cholesky(gram)
    ortho = lax.linalg.triangular_solve(lower, power.T, left_side=True, lower=True).T
    coeff = product(ortho.T, buffer)
    squares = lax.optimization_barrier(jnp.sum(coeff * coeff, axis=1))
    new_basis = coeff / jnp.sqrt(squares + epsilon)[:, None]
    new_momentum = buffer - (1.0 - decay_rate) * product(ortho, coeff)
    scale = step_size * math.sqrt(N / ROWS)
    new_weight = (weight.astype(jnp.float32) - scale * product(ortho, new_basis)).astype(jnp.bfloat16)
    blocks = inputs.reshape(-1, TOK_DEV, ROWS)

    def forward(block):
        return jnp.dot(block.astype(jnp.float32), new_weight.astype(jnp.float32), preferred_element_type=jnp.float32).astype(jnp.bfloat16)
    activations = lax.map(forward, blocks).reshape(TOKENS, N)
    return (new_momentum, new_basis, new_weight, activations)
```

```python
import functools
import math

import jax
import jax.numpy as jnp
from jax import lax
from jax.experimental import pallas as pl
from jax.experimental.pallas import tpu as pltpu
from jax.sharding import PartitionSpec as P

decay_rate = 0.8
step_size = 0.5
epsilon = 1e-06
highest = lax.Precision.HIGHEST
MESH = pl.DeviceIdType.MESH
LANES = 128
CHUNK = 16
SUB = 8

BUFFER_PLAN = (("yzx", 4), ("xzy", 4), ("zxy", 3), ("zyx", 2))
WEIGHT_PLAN = (("yzx", 4), ("xzy", 4), ("zxy", 3), ("zyx", 2))


def split_chunks(plan, chunks):
    total = sum(share for _, share in plan)
    parts, start, seen = [], 0, 0
    for order, share in plan:
        seen += share
        stop = (chunks * seen) // total
        if stop > start:
            parts.append((order, start, stop - start))
        start = stop
    return parts


class Mover:
    def __init__(self, buf, window, order, number, coords, depth, send_sem, recv_sem):
        self.buf, self.window, self.order, self.number = buf, window, order, number
        self.coords, self.depth = coords, depth
        self.send_sem, self.recv_sem = send_sem, recv_sem
        self.sent = []
        self.phase = 0

    def block(self, **fixed):
        done = self.order[: self.phase]
        index = []
        for axis in "zyxc":
            if axis in fixed:
                index.append(fixed[axis])
            elif axis in done:
                index.append(slice(None))
            else:
                index.append(self.coords[axis])
        return self.buf.at[tuple(index) + self.window]

    def copy(self, ref, slot, **target):
        where = dict(self.coords, **target)
        device = ((where["z"] * 2 + where["y"]) * 2 + where["x"]) * 2 + where["c"]
        return pltpu.make_async_remote_copy(
            src_ref=ref,
            dst_ref=ref,
            send_sem=self.send_sem.at[self.number, slot],
            recv_sem=self.recv_sem.at[self.number, slot],
            device_id={"fsdp": device},
            device_id_type=MESH,
        )

    def hops(self):
        axis = self.order[self.phase]
        base = self.order.index(axis) if axis != "z" else 4
        if axis == "z":
            return [(4 + k, (self.coords["z"] + k) % self.depth, (self.coords["z"] + self.depth - k) % self.depth)
                    for k in range(1, self.depth)]
        other = 1 - self.coords[axis]
        return [(base if base < 2 else 2, other, other)]

    def start(self):
        axis = self.order[self.phase]
        for slot, target, _ in self.hops():
            copy = self.copy(self.block(), slot, **{axis: target})
            copy.start()
            self.sent.append(copy)

    def finish(self):
        axis = self.order[self.phase]
        for slot, _, source in self.hops():
            self.copy(self.block(**{axis: source}), slot, **{axis: source}).wait_recv()
        self.phase += 1

    def to_sibling(self, last):
        axis = self.order[2]
        side = 1 - self.coords[axis] if last else self.coords[axis]
        copy = self.copy(self.block(**{axis: side}), 3 if last else 4, c=1 - self.coords["c"])
        copy.start()
        self.sent.append(copy)

    def from_sibling(self):
        axis, other = self.order[2], 1 - self.coords["c"]
        for side, slot in ((self.coords[axis], 4), (1 - self.coords[axis], 3)):
            self.copy(self.block(**{axis: side, "c": other}), slot, c=other).wait_recv()

    def drain(self):
        for copy in self.sent:
            copy.wait_send()


def gather_kernel(depth, rank, rows_local, has_power, *refs):
    (m_ref, g_ref, basis_ref, w_ref, power_ref, gathered, coeff_ref, ortho_ref, mine_ref, squares_ref,
     rows_buf, power_buf, send_sem, recv_sem, local_sem) = refs
    chunks = m_ref.shape[1] // CHUNK
    me = lax.axis_index("fsdp")
    coords = {"z": me // 8, "y": (me // 4) % 2, "x": (me // 2) % 2, "c": me % 2}
    here = (coords["z"], coords["y"], coords["x"], coords["c"])

    def number(z, y, x, c):
        return ((z * 2 + y) * 2 + x) * 2 + c

    partners = [number((coords["z"] + k) % depth, *here[1:]) for k in range(1, depth)]
    partners += [
        number(here[0], 1 - here[1], here[2], here[3]),
        number(here[0], here[1], 1 - here[2], here[3]),
        number(here[0], here[1], here[2], 1 - here[3]),
    ]
    barrier = pltpu.get_barrier_semaphore()
    for partner in partners:
        pl.semaphore_signal(barrier, inc=1, device_id={"fsdp": partner}, device_id_type=MESH)

    own = pltpu.make_async_copy(w_ref, gathered.at[here], local_sem)
    own.start()

    for row in range(rows_local):
        buffer = decay_rate * m_ref[row] + g_ref[row]
        rows_buf[here + (row,)] = buffer.astype(jnp.bfloat16)
        if has_power:
            power_buf[here + (pl.ds(row * SUB, SUB),)] = power_ref[pl.ds(row * SUB, SUB)]
        else:
            tile = [
                jnp.broadcast_to(
                    jnp.sum(buffer * basis_ref[pl.ds(k, m_ref.shape[1], stride=rank)], keepdims=True), (1, LANES)
                )
                for k in range(rank)
            ]
            tile += [jnp.zeros((1, LANES), jnp.float32)] * (SUB - rank)
            power_buf[here + (pl.ds(row * SUB, SUB),)] = jnp.concatenate(tile, axis=0)
    pl.semaphore_wait(barrier, len(partners))

    def mover(buf, window, order, count):
        return Mover(buf, window, order, count, coords, depth, send_sem, recv_sem)

    def windows(plan):
        return [
            (order, (slice(None), pl.ds(first * CHUNK, count * CHUNK), slice(None)))
            for order, first, count in split_chunks(plan, chunks)
        ]

    early = [mover(power_buf, (slice(None), slice(None)), "zxy", 0)]
    for order, window in windows(BUFFER_PLAN):
        early.append(mover(rows_buf, window, order, len(early)))
    late = []
    for order, window in windows(WEIGHT_PLAN):
        late.append(mover(gathered, window, order, len(early) + len(late)))

    def advance(movers):
        for part in movers:
            part.finish()
            if part.phase == 2:
                part.to_sibling(False)
            if part.phase < 3:
                part.start()
            else:
                part.to_sibling(True)

    for part in early:
        part.start()
    own.wait()
    for part in late:
        part.start()
    advance(early)
    advance(late)
    advance(early)
    advance(late)
    advance(early)
    for part in early:
        part.from_sibling()

    devices = [(z, y, x, c) for z in range(depth) for y in range(2) for x in range(2) for c in range(2)]
    tiles = [power_buf[d + (pl.ds(row * SUB, SUB),)] for d in devices for row in range(rows_local)]
    gram = []
    for l in range(rank):
        total = jnp.zeros((SUB, LANES), jnp.float32)
        for tile in tiles:
            total = total + tile * tile[l : l + 1]
        gram.append(total)
    lower = [[None] * rank for _ in range(rank)]
    inverse = [None] * rank
    for l in range(rank):
        value = gram[l][l : l + 1]
        for j in range(l):
            value = value - lower[l][j] * lower[l][j]
        lower[l][l] = jnp.sqrt(value)
        inverse[l] = 1.0 / lower[l][l]
        for k in range(l + 1, rank):
            value = gram[l][k : k + 1]
            for j in range(l):
                value = value - lower[k][j] * lower[l][j]
            lower[k][l] = value * inverse[l]

    def solve(right):
        found = []
        for k in range(rank):
            value = right[k]
            for j in range(k):
                value = value - lower[k][j] * found[j]
            found.append(value * inverse[k])
        return found

    filler = [jnp.zeros((1, LANES), jnp.float32)] * (SUB - rank)
    for i, tile in enumerate(tiles):
        found = solve([tile[k : k + 1] for k in range(rank)])
        ortho_ref[pl.ds(i * SUB, SUB)] = jnp.concatenate(found + filler, axis=0)
    for row in range(rows_local):
        tile = power_buf[here + (pl.ds(row * SUB, SUB),)]
        found = solve([tile[k : k + 1] for k in range(rank)])
        mine_ref[pl.ds(row * SUB, SUB)] = jnp.concatenate(found + filler, axis=0)

    def one_chunk(i, squares):
        at = pl.ds(pl.multiple_of(i * CHUNK, CHUNK), CHUNK)
        raw = [jnp.zeros((CHUNK, LANES), jnp.float32) for _ in range(rank)]
        for d in devices:
            for row in range(rows_local):
                values = rows_buf[d + (row, at)].astype(jnp.float32)
                for k in range(rank):
                    raw[k] = raw[k] + values * power_buf[d + (pl.ds(row * SUB + k, 1),)]
        found = solve(raw)
        for k in range(rank):
            coeff_ref[k, at] = found[k]
        return tuple(squares[k] + found[k] * found[k] for k in range(rank))

    squares = lax.fori_loop(
        0, chunks, one_chunk, tuple(jnp.zeros((CHUNK, LANES), jnp.float32) for _ in range(rank))
    )
    squares_ref[...] = jnp.concatenate(
        [jnp.broadcast_to(jnp.sum(squares[k], keepdims=True), (1, LANES)) for k in range(rank)] + filler, axis=0
    )

    advance(late)
    for part in late:
        part.from_sibling()
    for part in early + late:
        part.drain()


def apply_kernel(scale, rank, rows_local, ortho_ref, mine_ref, squares_ref, x_ref, w_all_ref, coeff_ref, m_ref, g_ref,
                 w_ref, act_ref, nm_ref, nb_ref, nw_ref, spread):
    rows = w_all_ref.shape[0]
    coeff = [coeff_ref[k] for k in range(rank)]
    basis = []
    for k in range(rank):
        norm = jnp.sqrt(squares_ref[k : k + 1] + epsilon)
        basis.append(coeff[k] * (1.0 / norm))
        nb_ref[pl.ds(k, CHUNK, stride=rank)] = basis[k]

    def lowered(weight, ref, row):
        change = ref[pl.ds(row * SUB, 1)] * basis[0]
        for k in range(1, rank):
            change = change + ref[pl.ds(row * SUB + k, 1)] * basis[k]
        return weight.astype(jnp.float32) - scale * change

    for row in range(rows_local):
        nw_ref[row] = lowered(w_ref[row], mine_ref, row).astype(jnp.bfloat16)
        feedback = mine_ref[pl.ds(row * SUB, 1)] * coeff[0]
        for k in range(1, rank):
            feedback = feedback + mine_ref[pl.ds(row * SUB + k, 1)] * coeff[k]
        nm_ref[row] = decay_rate * m_ref[row] + g_ref[row] - (1.0 - decay_rate) * feedback
    for row in range(rows):
        spread[pl.ds(row * CHUNK, CHUNK)] = lowered(w_all_ref[row], ortho_ref, row)
    weights = jnp.concatenate(
        [spread[pl.ds(j, rows, stride=CHUNK)].astype(jnp.bfloat16) for j in range(CHUNK)], axis=1
    )
    act_ref[...] = jnp.dot(x_ref[...], weights, preferred_element_type=jnp.float32).astype(jnp.bfloat16)


def on_device(fsdp, tp, momentum, gradient, basis, weight, inputs):
    rows_local, width = momentum.shape
    rank = basis.shape[0]
    rows = rows_local * fsdp
    tokens = inputs.shape[0]
    depth = fsdp // 8
    assert depth * 8 == fsdp and rank <= SUB
    scale = step_size * math.sqrt(width * tp / rows)
    block = CHUNK * LANES
    padded = -(-width // block) * block
    groups = padded // LANES
    chunks = groups // CHUNK

    def dense(array):
        if padded != width:
            array = jnp.pad(array, ((0, 0), (0, padded - width)))
        return array.reshape(array.shape[0], groups, LANES)

    m, g, w = dense(momentum), dense(gradient), dense(weight)
    b = dense(basis).transpose(1, 0, 2).reshape(groups * rank, LANES)
    if tp > 1:
        buffer = decay_rate * momentum + gradient
        power = lax.psum(
            lax.dot_general(buffer, basis, (((1,), (1,)), ((), ())), precision=highest,
                            preferred_element_type=jnp.float32), "tp")
        power = jnp.pad(power, ((0, 0), (0, SUB - rank))).reshape(rows_local * SUB, 1)
        power = jnp.broadcast_to(power, (rows_local * SUB, LANES))
    else:
        power = jnp.zeros((SUB, LANES), jnp.float32)

    vmem = pl.BlockSpec(memory_space=pltpu.VMEM)
    anywhere = pl.BlockSpec(memory_space=pl.ANY)
    parts = 1 + len(split_chunks(BUFFER_PLAN, chunks)) + len(split_chunks(WEIGHT_PLAN, chunks))
    f32, bf16 = jnp.float32, jnp.bfloat16
    gathered, coeff, ortho, mine, squares = pl.pallas_call(
        functools.partial(gather_kernel, depth, rank, rows_local, tp > 1),
        out_shape=(
            jax.ShapeDtypeStruct((depth, 2, 2, 2, rows_local, groups, LANES), bf16),
            jax.ShapeDtypeStruct((rank, groups, LANES), f32),
            jax.ShapeDtypeStruct((rows * SUB, LANES), f32),
            jax.ShapeDtypeStruct((rows_local * SUB, LANES), f32),
            jax.ShapeDtypeStruct((SUB, LANES), f32),
        ),
        in_specs=[vmem] * 5,
        out_specs=(anywhere, vmem, vmem, vmem, vmem),
        scratch_shapes=[
            pltpu.VMEM((depth, 2, 2, 2, rows_local, groups, LANES), bf16),
            pltpu.VMEM((depth, 2, 2, 2, rows_local * SUB, LANES), f32),
            pltpu.SemaphoreType.DMA((parts, 4 + depth)),
            pltpu.SemaphoreType.DMA((parts, 4 + depth)),
            pltpu.SemaphoreType.DMA,
        ],
        compiler_params=pltpu.CompilerParams(
            collective_id=0, has_side_effects=True, vmem_limit_bytes=32 * 1024 * 1024
        ),
        name="gather_rows",
    )(m, g, b, w, power)

    if tp > 1:
        squares = lax.psum(squares, "tp")
    w_all = gathered.reshape(rows, groups, LANES)

    def whole(array):
        return pl.BlockSpec(array.shape, lambda i: (0,) * array.ndim)

    def sliced(lead):
        return pl.BlockSpec((lead, CHUNK, LANES), lambda i: (0, i, 0))

    act, nm, nb, nw = pl.pallas_call(
        functools.partial(apply_kernel, scale, rank, rows_local),
        grid=(chunks,),
        out_shape=(
            jax.ShapeDtypeStruct((tokens, padded), bf16),
            jax.ShapeDtypeStruct((rows_local, groups, LANES), f32),
            jax.ShapeDtypeStruct((groups * rank, LANES), f32),
            jax.ShapeDtypeStruct((rows_local, groups, LANES), bf16),
        ),
        in_specs=[
            whole(ortho), whole(mine), whole(squares), whole(inputs),
            sliced(rows), sliced(rank), sliced(rows_local), sliced(rows_local), sliced(rows_local),
        ],
        out_specs=(
            pl.BlockSpec((tokens, block), lambda i: (0, i)),
            sliced(rows_local),
            pl.BlockSpec((CHUNK * rank, LANES), lambda i: (i, 0)),
            sliced(rows_local),
        ),
        scratch_shapes=[pltpu.VMEM((rows * CHUNK, LANES), f32)],
        compiler_params=pltpu.CompilerParams(vmem_limit_bytes=32 * 1024 * 1024),
        name="apply_update",
    )(ortho, mine, squares, inputs, w_all, coeff, m, g, w)

    def flat(array):
        return array.reshape(array.shape[0], padded)[:, :width]

    new_basis = flat(nb.reshape(groups, rank, LANES).transpose(1, 0, 2))
    return flat(nm), new_basis, flat(nw), act[:, :width]


def solution(mesh):
    return jax.shard_map(
        functools.partial(on_device, mesh.shape["fsdp"], mesh.shape["tp"]),
        mesh=mesh,
        in_specs=(
            P("fsdp", "tp"),
            P("fsdp", "tp"),
            P(None, "tp"),
            P("fsdp", "tp"),
            P("fsdp", None),
        ),
        out_specs=(P("fsdp", "tp"), P(None, "tp"), P("fsdp", "tp"), P("fsdp", "tp")),
        check_vma=False,
    )
```

```python
import functools
import math

import jax
import jax.numpy as jnp
from jax import lax
from jax.experimental import pallas as pl
from jax.experimental.pallas import tpu as pltpu
from jax.sharding import PartitionSpec as P

decay_rate = 0.8
step_size = 0.5
epsilon = 1e-06
highest = lax.Precision.HIGHEST
MESH = pl.DeviceIdType.MESH
LANES = 128
CHUNK = 16
PITCH = 24
SUB = 8

WEIGHT_PLAN = (("yzx", 4), ("xzy", 4), ("zxy", 3), ("zyx", 2))


def split_chunks(plan, chunks):
    total = sum(share for _, share in plan)
    parts, start, seen = [], 0, 0
    for order, share in plan:
        seen += share
        stop = (chunks * seen) // total
        if stop > start:
            parts.append((order, start, stop - start))
        start = stop
    return parts


class Mover:
    def __init__(self, buf, window, order, number, coords, depth, send_sem, recv_sem):
        self.buf, self.window, self.order, self.number = buf, window, order, number
        self.coords, self.depth = coords, depth
        self.send_sem, self.recv_sem = send_sem, recv_sem
        self.sent = []
        self.phase = 0

    def block(self, **fixed):
        done = self.order[: self.phase]
        index = []
        for axis in "zyxc":
            if axis in fixed:
                index.append(fixed[axis])
            elif axis in done:
                index.append(slice(None))
            else:
                index.append(self.coords[axis])
        return self.buf.at[tuple(index) + self.window]

    def copy(self, ref, slot, **target):
        where = dict(self.coords, **target)
        device = ((where["z"] * 2 + where["y"]) * 2 + where["x"]) * 2 + where["c"]
        return pltpu.make_async_remote_copy(
            src_ref=ref,
            dst_ref=ref,
            send_sem=self.send_sem.at[self.number, slot],
            recv_sem=self.recv_sem.at[self.number, slot],
            device_id={"fsdp": device},
            device_id_type=MESH,
        )

    def hops(self):
        axis = self.order[self.phase]
        base = self.order.index(axis) if axis != "z" else 4
        if axis == "z":
            return [(4 + k, (self.coords["z"] + k) % self.depth, (self.coords["z"] + self.depth - k) % self.depth)
                    for k in range(1, self.depth)]
        other = 1 - self.coords[axis]
        return [(base if base < 2 else 2, other, other)]

    def start(self):
        axis = self.order[self.phase]
        for slot, target, _ in self.hops():
            copy = self.copy(self.block(), slot, **{axis: target})
            copy.start()
            self.sent.append(copy)

    def finish(self):
        axis = self.order[self.phase]
        for slot, _, source in self.hops():
            self.copy(self.block(**{axis: source}), slot, **{axis: source}).wait_recv()
        self.phase += 1

    def to_sibling(self, last):
        axis = self.order[2]
        side = 1 - self.coords[axis] if last else self.coords[axis]
        copy = self.copy(self.block(**{axis: side}), 3 if last else 4, c=1 - self.coords["c"])
        copy.start()
        self.sent.append(copy)

    def from_sibling(self):
        axis, other = self.order[2], 1 - self.coords["c"]
        for side, slot in ((self.coords[axis], 4), (1 - self.coords[axis], 3)):
            self.copy(self.block(**{axis: side, "c": other}), slot, c=other).wait_recv()

    def drain(self):
        for copy in self.sent:
            copy.wait_send()


def gather_kernel(depth, rank, rows_local, unit, has_power, *refs):
    (m_hbm, g_hbm, basis_hbm, xt_hbm, w_ref, power_ref, gathered, coeff_ref, buffer_ref, x_ref, ortho_ref, mine_ref,
     squares_ref, m_ref, g_ref, basis_ref, xt_ref, sums, from_c, from_x, from_y, from_z, coeff_buf, power_buf,
     send_sem, recv_sem, sums_send, sums_recv, local_sem) = refs
    groups = m_ref.shape[1]
    chunks = groups // CHUNK
    me = lax.axis_index("fsdp")
    coords = {"z": me // 8, "y": (me // 4) % 2, "x": (me // 2) % 2, "c": me % 2}
    here = (coords["z"], coords["y"], coords["x"], coords["c"])

    def number(z, y, x, c):
        return ((z * 2 + y) * 2 + x) * 2 + c

    partners = [number((coords["z"] + k) % depth, *here[1:]) for k in range(1, depth)]
    over_y = number(here[0], 1 - here[1], here[2], here[3])
    over_x = number(here[0], here[1], 1 - here[2], here[3])
    sibling = number(here[0], here[1], here[2], 1 - here[3])
    partners += [over_y, over_x, sibling]
    barrier = pltpu.get_barrier_semaphore()
    for partner in partners:
        pl.semaphore_signal(barrier, inc=1, device_id={"fsdp": partner}, device_id_type=MESH)

    loads = [
        pltpu.make_async_copy(source, target, local_sem.at[i])
        for i, (source, target) in enumerate(
            ((w_ref, gathered.at[here]), (m_hbm, m_ref), (g_hbm, g_ref), (basis_hbm, basis_ref), (xt_hbm, xt_ref))
        )
    ]
    for load in loads:
        load.start()
    for load in loads[1:4]:
        load.wait()

    for row in range(rows_local):
        buffer_ref[row] = decay_rate * m_ref[row] + g_ref[row]
        if has_power:
            power_buf[here + (pl.ds(row * SUB, SUB),)] = power_ref[pl.ds(row * SUB, SUB)]
        else:
            tile = [
                jnp.broadcast_to(
                    jnp.sum(buffer_ref[row] * basis_ref[pl.ds(k, groups, stride=rank)], keepdims=True), (1, LANES)
                )
                for k in range(rank)
            ]
            tile += [jnp.zeros((1, LANES), jnp.float32)] * (SUB - rank)
            power_buf[here + (pl.ds(row * SUB, SUB),)] = jnp.concatenate(tile, axis=0)

    devices = [(z, y, x, c) for z in range(depth) for y in range(2) for x in range(2) for c in range(2)]
    owners = groups // unit
    own_power = [power_buf[here + (pl.ds(row * SUB, SUB),)] for row in range(rows_local)]
    for i, d in enumerate(devices):
        for k in range(rank):
            at = pl.ds(k * unit, unit)
            if i >= owners:
                sums[d + (at,)] = jnp.zeros((unit, LANES), jnp.float32)
                continue
            term = jnp.zeros((unit, LANES), jnp.float32)
            for row in range(rows_local):
                term = term + own_power[row][k : k + 1] * buffer_ref[row, pl.ds(i * unit, unit)]
            sums[d + (at,)] = term
    pl.semaphore_wait(barrier, len(partners))

    def mover(buf, window, order, count):
        return Mover(buf, window, order, count, coords, depth, send_sem, recv_sem)

    everything = (slice(None), slice(None))
    power_part = mover(power_buf, everything, "zxy", 0)
    coeff_part = mover(coeff_buf, everything, "zxy", 1)
    late = []
    for order, first, count in split_chunks(WEIGHT_PLAN, chunks):
        window = (slice(None), pl.ds(first * CHUNK, count * CHUNK), slice(None))
        late.append(mover(gathered, window, order, 2 + len(late)))

    def advance(movers):
        for part in movers:
            part.finish()
            if part.phase == 2:
                part.to_sibling(False)
            if part.phase < 3:
                part.start()
            else:
                part.to_sibling(True)

    def sums_copy(source, target, slot, device):
        return pltpu.make_async_remote_copy(
            src_ref=source, dst_ref=target, send_sem=sums_send.at[slot], recv_sem=sums_recv.at[slot],
            device_id={"fsdp": device}, device_id_type=MESH,
        )

    z, y, x, c = here
    all_of = slice(None)
    copy_c = sums_copy(sums.at[all_of, all_of, all_of, 1 - c], from_c, 0, sibling)
    copy_x = sums_copy(sums.at[all_of, all_of, 1 - x, c], from_x, 1, over_x)
    copy_y = sums_copy(sums.at[all_of, 1 - y, x, c], from_y, 2, over_y)
    copy_z = [
        sums_copy(sums.at[(z + k) % depth, y, x, c], from_z.at[k - 1], 2 + k,
                  number((z + k) % depth, y, x, c))
        for k in range(1, depth)
    ]

    power_part.start()
    copy_c.start()
    loads[0].wait()
    for part in late:
        part.start()
    copy_c.wait_recv()
    for i in range(depth):
        for j in range(2):
            for h in range(2):
                sums[i, j, h, c] = sums[i, j, h, c] + from_c[i, j, h]
    copy_x.start()
    advance([power_part])
    loads[4].wait()
    x_ref[...] = jnp.transpose(xt_ref[...].astype(jnp.float32)).astype(jnp.bfloat16)
    copy_x.wait_recv()
    for i in range(depth):
        for j in range(2):
            sums[i, j, x, c] = sums[i, j, x, c] + from_x[i, j]
    copy_y.start()
    advance([power_part])
    advance(late)
    copy_y.wait_recv()
    for i in range(depth):
        sums[i, y, x, c] = sums[i, y, x, c] + from_y[i]
    for copy in copy_z:
        copy.start()
    advance([power_part])
    power_part.from_sibling()

    tiles = [power_buf[d + (pl.ds(row * SUB, SUB),)] for d in devices for row in range(rows_local)]
    gram = []
    for l in range(rank):
        total = jnp.zeros((SUB, LANES), jnp.float32)
        for tile in tiles:
            total = total + tile * tile[l : l + 1]
        gram.append(total)
    lower = [[None] * rank for _ in range(rank)]
    inverse = [None] * rank
    for l in range(rank):
        value = gram[l][l : l + 1]
        for j in range(l):
            value = value - lower[l][j] * lower[l][j]
        lower[l][l] = jnp.sqrt(value)
        inverse[l] = 1.0 / lower[l][l]
        for k in range(l + 1, rank):
            value = gram[l][k : k + 1]
            for j in range(l):
                value = value - lower[k][j] * lower[l][j]
            lower[k][l] = value * inverse[l]

    def solve(right):
        found = []
        for k in range(rank):
            value = right[k]
            for j in range(k):
                value = value - lower[k][j] * found[j]
            found.append(value * inverse[k])
        return found

    for copy in copy_z:
        copy.wait_recv()
    total = sums[here]
    for k in range(1, depth):
        total = total + from_z[k - 1]
    coeff_buf[here] = jnp.concatenate(solve([total[k * unit : (k + 1) * unit] for k in range(rank)]), axis=0)
    coeff_part.start()

    filler = [jnp.zeros((1, LANES), jnp.float32)] * (SUB - rank)
    for i, tile in enumerate(tiles):
        found = solve([tile[k : k + 1] for k in range(rank)])
        ortho_ref[pl.ds(i * SUB, SUB)] = jnp.concatenate(found + filler, axis=0)
    for row in range(rows_local):
        tile = own_power[row]
        found = solve([tile[k : k + 1] for k in range(rank)])
        mine_ref[pl.ds(row * SUB, SUB)] = jnp.concatenate(found + filler, axis=0)

    advance([coeff_part])
    advance(late)
    advance([coeff_part])
    advance([coeff_part])
    advance(late)
    coeff_part.from_sibling()
    squares = [jnp.zeros((unit, LANES), jnp.float32) for _ in range(rank)]
    for i in range(owners):
        slot = coeff_buf[devices[i]]
        for k in range(rank):
            values = slot[k * unit : (k + 1) * unit]
            coeff_ref[k, pl.ds(i * unit, unit)] = values
            squares[k] = squares[k] + values * values
    squares_ref[...] = jnp.concatenate(
        [jnp.broadcast_to(jnp.sum(squares[k], keepdims=True), (1, LANES)) for k in range(rank)] + filler, axis=0
    )

    for part in late:
        part.from_sibling()
    for part in [power_part, coeff_part] + late:
        part.drain()
    for copy in [copy_c, copy_x, copy_y] + copy_z:
        copy.wait_send()


def apply_kernel(scale, rank, rows_local, ortho_ref, mine_ref, squares_ref, x_ref, w_all_ref, coeff_ref, buffer_ref,
                 w_ref, act_ref, nm_ref, nb_ref, nw_ref, spread):
    rows = w_all_ref.shape[0]
    coeff = [coeff_ref[k] for k in range(rank)]
    basis = []
    for k in range(rank):
        norm = jnp.sqrt(squares_ref[k : k + 1] + epsilon)
        basis.append(coeff[k] * (1.0 / norm))
        nb_ref[pl.ds(k, CHUNK, stride=rank)] = basis[k]

    def lowered(weight, ref, row):
        change = ref[pl.ds(row * SUB, 1)] * basis[0]
        for k in range(1, rank):
            change = change + ref[pl.ds(row * SUB + k, 1)] * basis[k]
        return weight.astype(jnp.float32) - scale * change

    for row in range(rows_local):
        nw_ref[row] = lowered(w_ref[row], mine_ref, row).astype(jnp.bfloat16)
        feedback = mine_ref[pl.ds(row * SUB, 1)] * coeff[0]
        for k in range(1, rank):
            feedback = feedback + mine_ref[pl.ds(row * SUB + k, 1)] * coeff[k]
        nm_ref[row] = buffer_ref[row] - (1.0 - decay_rate) * feedback
    for row in range(rows):
        spread[pl.ds(row * PITCH, CHUNK)] = lowered(w_all_ref[row], ortho_ref, row)
    for j in range(0, CHUNK, 2):
        weights = jnp.concatenate(
            [spread[pl.ds(j + i, rows, stride=PITCH)].astype(jnp.bfloat16) for i in range(2)], axis=1
        )
        act_ref[:, pl.ds(j * LANES, 2 * LANES)] = jnp.dot(
            x_ref[...], weights, preferred_element_type=jnp.float32
        ).astype(jnp.bfloat16)


def on_device(fsdp, tp, momentum, gradient, basis, weight, inputs):
    rows_local, width = momentum.shape
    rank = basis.shape[0]
    rows = rows_local * fsdp
    tokens = inputs.shape[0]
    depth = fsdp // 8
    assert depth * 8 == fsdp and rank <= SUB
    scale = step_size * math.sqrt(width * tp / rows)
    block = CHUNK * LANES
    padded = -(-width // block) * block
    groups = padded // LANES
    chunks = groups // CHUNK

    def dense(array):
        if padded != width:
            array = jnp.pad(array, ((0, 0), (0, padded - width)))
        return array.reshape(array.shape[0], groups, LANES)

    m, g, w = dense(momentum), dense(gradient), dense(weight)
    b = dense(basis).transpose(1, 0, 2).reshape(groups * rank, LANES)
    if tp > 1:
        buffer = decay_rate * momentum + gradient
        power = lax.psum(
            lax.dot_general(buffer, basis, (((1,), (1,)), ((), ())), precision=highest,
                            preferred_element_type=jnp.float32), "tp")
        power = jnp.pad(power, ((0, 0), (0, SUB - rank))).reshape(rows_local * SUB, 1)
        power = jnp.broadcast_to(power, (rows_local * SUB, LANES))
    else:
        power = jnp.zeros((SUB, LANES), jnp.float32)

    vmem = pl.BlockSpec(memory_space=pltpu.VMEM)
    hbm = pl.BlockSpec(memory_space=pltpu.HBM)
    anywhere = pl.BlockSpec(memory_space=pl.ANY)
    unit = SUB * -(-groups // (SUB * fsdp))
    assert groups % unit == 0
    parts = 2 + len(split_chunks(WEIGHT_PLAN, chunks))
    f32, bf16 = jnp.float32, jnp.bfloat16
    slot = (rank * unit, LANES)
    gathered, coeff, buffer, x, ortho, mine, squares = pl.pallas_call(
        functools.partial(gather_kernel, depth, rank, rows_local, unit, tp > 1),
        out_shape=(
            jax.ShapeDtypeStruct((depth, 2, 2, 2, rows_local, groups, LANES), bf16),
            jax.ShapeDtypeStruct((rank, groups, LANES), f32),
            jax.ShapeDtypeStruct((rows_local, groups, LANES), f32),
            jax.ShapeDtypeStruct((tokens, rows), bf16),
            jax.ShapeDtypeStruct((rows * SUB, LANES), f32),
            jax.ShapeDtypeStruct((rows_local * SUB, LANES), f32),
            jax.ShapeDtypeStruct((SUB, LANES), f32),
        ),
        in_specs=[hbm] * 4 + [vmem] * 2,
        out_specs=(anywhere,) + (vmem,) * 6,
        scratch_shapes=[
            pltpu.VMEM(m.shape, f32),
            pltpu.VMEM(g.shape, f32),
            pltpu.VMEM(b.shape, f32),
            pltpu.VMEM((rows, tokens), bf16),
            pltpu.VMEM((depth, 2, 2, 2) + slot, f32),
            pltpu.VMEM((depth, 2, 2) + slot, f32),
            pltpu.VMEM((depth, 2) + slot, f32),
            pltpu.VMEM((depth,) + slot, f32),
            pltpu.VMEM((depth,) + slot, f32),
            pltpu.VMEM((depth, 2, 2, 2) + slot, f32),
            pltpu.VMEM((depth, 2, 2, 2, rows_local * SUB, LANES), f32),
            pltpu.SemaphoreType.DMA((parts, 4 + depth)),
            pltpu.SemaphoreType.DMA((parts, 4 + depth)),
            pltpu.SemaphoreType.DMA((2 + depth,)),
            pltpu.SemaphoreType.DMA((2 + depth,)),
            pltpu.SemaphoreType.DMA((5,)),
        ],
        compiler_params=pltpu.CompilerParams(
            collective_id=0, has_side_effects=True, vmem_limit_bytes=32 * 1024 * 1024
        ),
        name="gather_rows",
    )(m, g, b, inputs.T, w, power)

    if tp > 1:
        squares = lax.psum(squares, "tp")
    w_all = gathered.reshape(rows, groups, LANES)

    def whole(array):
        return pl.BlockSpec(array.shape, lambda i: (0,) * array.ndim)

    def sliced(lead):
        return pl.BlockSpec((lead, CHUNK, LANES), lambda i: (0, i, 0))

    act, nm, nb, nw = pl.pallas_call(
        functools.partial(apply_kernel, scale, rank, rows_local),
        grid=(chunks,),
        out_shape=(
            jax.ShapeDtypeStruct((tokens, padded), bf16),
            jax.ShapeDtypeStruct((rows_local, groups, LANES), f32),
            jax.ShapeDtypeStruct((groups * rank, LANES), f32),
            jax.ShapeDtypeStruct((rows_local, groups, LANES), bf16),
        ),
        in_specs=[
            whole(ortho), whole(mine), whole(squares), whole(x),
            sliced(rows), sliced(rank), sliced(rows_local), sliced(rows_local),
        ],
        out_specs=(
            pl.BlockSpec((tokens, block), lambda i: (0, i)),
            sliced(rows_local),
            pl.BlockSpec((CHUNK * rank, LANES), lambda i: (i, 0)),
            sliced(rows_local),
        ),
        scratch_shapes=[pltpu.VMEM((rows * PITCH, LANES), f32)],
        compiler_params=pltpu.CompilerParams(vmem_limit_bytes=32 * 1024 * 1024),
        name="apply_update",
    )(ortho, mine, squares, x, w_all, coeff, buffer, w)

    def flat(array):
        return array.reshape(array.shape[0], padded)[:, :width]

    new_basis = flat(nb.reshape(groups, rank, LANES).transpose(1, 0, 2))
    return flat(nm), new_basis, flat(nw), act[:, :width]


def solution(mesh):
    return jax.shard_map(
        functools.partial(on_device, mesh.shape["fsdp"], mesh.shape["tp"]),
        mesh=mesh,
        in_specs=(
            P("fsdp", "tp"),
            P("fsdp", "tp"),
            P(None, "tp"),
            P("fsdp", "tp"),
            P("fsdp", None),
        ),
        out_specs=(P("fsdp", "tp"), P(None, "tp"), P("fsdp", "tp"), P("fsdp", "tp")),
        check_vma=False,
    )
```

```python
import functools
import math

import jax
import jax.numpy as jnp
from jax import lax
from jax.experimental import pallas as pl
from jax.experimental.pallas import tpu as pltpu
from jax.sharding import PartitionSpec as P

decay_rate = 0.8
step_size = 0.5
epsilon = 1e-06
highest = lax.Precision.HIGHEST
MESH = pl.DeviceIdType.MESH
LANES = 128
PLANE = [(y, x, c) for y in range(2) for x in range(2) for c in range(2)][1:]
CHUNK = 16
PITCH = 24
SUB = 8

WEIGHT_PLAN = (("yzx", 3), ("xzy", 3), ("zxy", 4), ("zyx", 3))


def split_chunks(plan, chunks):
    total = sum(share for _, share in plan)
    parts, start, seen = [], 0, 0
    for order, share in plan:
        seen += share
        stop = (chunks * seen) // total
        if stop > start:
            parts.append((order, start, stop - start))
        start = stop
    return parts


class Mover:
    def __init__(self, buf, window, order, number, coords, depth, send_sem, recv_sem):
        self.buf, self.window, self.order, self.number = buf, window, order, number
        self.coords, self.depth = coords, depth
        self.send_sem, self.recv_sem = send_sem, recv_sem
        self.sent = []
        self.phase = 0

    def block(self, **fixed):
        done = self.order[: self.phase]
        index = []
        for axis in "zyxc":
            if axis in fixed:
                index.append(fixed[axis])
            elif axis in done:
                index.append(slice(None))
            else:
                index.append(self.coords[axis])
        return self.buf.at[tuple(index) + self.window]

    def copy(self, ref, slot, **target):
        where = dict(self.coords, **target)
        device = ((where["z"] * 2 + where["y"]) * 2 + where["x"]) * 2 + where["c"]
        return pltpu.make_async_remote_copy(
            src_ref=ref,
            dst_ref=ref,
            send_sem=self.send_sem.at[self.number, slot],
            recv_sem=self.recv_sem.at[self.number, slot],
            device_id={"fsdp": device},
            device_id_type=MESH,
        )

    def hops(self):
        axis = self.order[self.phase]
        base = self.order.index(axis) if axis != "z" else 4
        if axis == "z":
            return [(4 + k, (self.coords["z"] + k) % self.depth, (self.coords["z"] + self.depth - k) % self.depth)
                    for k in range(1, self.depth)]
        other = 1 - self.coords[axis]
        return [(base if base < 2 else 2, other, other)]

    def start(self):
        axis = self.order[self.phase]
        for slot, target, _ in self.hops():
            copy = self.copy(self.block(), slot, **{axis: target})
            copy.start()
            self.sent.append(copy)

    def finish(self):
        axis = self.order[self.phase]
        for slot, _, source in self.hops():
            self.copy(self.block(**{axis: source}), slot, **{axis: source}).wait_recv()
        self.phase += 1

    def to_sibling(self, last):
        axis = self.order[2]
        side = 1 - self.coords[axis] if last else self.coords[axis]
        copy = self.copy(self.block(**{axis: side}), 3 if last else 4, c=1 - self.coords["c"])
        copy.start()
        self.sent.append(copy)

    def from_sibling(self):
        axis, other = self.order[2], 1 - self.coords["c"]
        for side, slot in ((self.coords[axis], 4), (1 - self.coords[axis], 3)):
            self.copy(self.block(**{axis: side, "c": other}), slot, c=other).wait_recv()

    def drain(self):
        for copy in self.sent:
            copy.wait_send()


def gather_kernel(depth, rank, rows_local, unit, has_power, *refs):
    (m_hbm, g_hbm, basis_hbm, xt_hbm, w_ref, power_ref, gathered, coeff_ref, buffer_ref, x_ref, ortho_ref, mine_ref,
     squares_ref, m_ref, g_ref, basis_ref, xt_ref, sums, from_plane, z_sums, from_z, coeff_buf, power_buf,
     send_sem, recv_sem, local_sem) = refs
    groups = m_ref.shape[1]
    chunks = groups // CHUNK
    me = lax.axis_index("fsdp")
    coords = {"z": me // 8, "y": (me // 4) % 2, "x": (me // 2) % 2, "c": me % 2}
    here = (coords["z"], coords["y"], coords["x"], coords["c"])

    def number(z, y, x, c):
        return ((z * 2 + y) * 2 + x) * 2 + c

    z, y, x, c = here
    peers = [((y + dy) % 2, (x + dx) % 2, (c + dc) % 2) for dy, dx, dc in PLANE]
    partners = [number((z + k) % depth, y, x, c) for k in range(1, depth)]
    partners += [number(z, *peer) for peer in peers]
    barrier = pltpu.get_barrier_semaphore()
    for partner in partners:
        pl.semaphore_signal(barrier, inc=1, device_id={"fsdp": partner}, device_id_type=MESH)

    loads = [
        pltpu.make_async_copy(source, target, local_sem.at[i])
        for i, (source, target) in enumerate(
            ((w_ref, gathered.at[here]), (m_hbm, m_ref), (g_hbm, g_ref), (basis_hbm, basis_ref), (xt_hbm, xt_ref))
        )
    ]
    for load in loads:
        load.start()
    for load in loads[1:4]:
        load.wait()

    for row in range(rows_local):
        buffer_ref[row] = decay_rate * m_ref[row] + g_ref[row]
        if has_power:
            power_buf[here + (pl.ds(row * SUB, SUB),)] = power_ref[pl.ds(row * SUB, SUB)]
        else:
            tile = [
                jnp.broadcast_to(
                    jnp.sum(buffer_ref[row] * basis_ref[pl.ds(k, groups, stride=rank)], keepdims=True), (1, LANES)
                )
                for k in range(rank)
            ]
            tile += [jnp.zeros((1, LANES), jnp.float32)] * (SUB - rank)
            power_buf[here + (pl.ds(row * SUB, SUB),)] = jnp.concatenate(tile, axis=0)

    devices = [(z, y, x, c) for z in range(depth) for y in range(2) for x in range(2) for c in range(2)]
    owners = groups // unit
    own_power = [power_buf[here + (pl.ds(row * SUB, SUB),)] for row in range(rows_local)]
    for i, d in enumerate(devices):
        if i >= owners:
            sums[d] = jnp.zeros((rank * unit, LANES), jnp.bfloat16)
            continue
        terms = []
        for k in range(rank):
            term = jnp.zeros((unit, LANES), jnp.float32)
            for row in range(rows_local):
                term = term + own_power[row][k : k + 1] * buffer_ref[row, pl.ds(i * unit, unit)]
            terms.append(term)
        sums[d] = jnp.concatenate(terms, axis=0).astype(jnp.bfloat16)
    pl.semaphore_wait(barrier, len(partners))

    def mover(buf, window, order, count):
        return Mover(buf, window, order, count, coords, depth, send_sem, recv_sem)

    late = []
    for order, first, count in split_chunks(WEIGHT_PLAN, chunks):
        window = (slice(None), pl.ds(first * CHUNK, count * CHUNK), slice(None))
        late.append(mover(gathered, window, order, 3 + len(late)))

    def advance(movers):
        for part in movers:
            part.finish()
            if part.phase == 2:
                part.to_sibling(False)
            if part.phase < 3:
                part.start()
            else:
                part.to_sibling(True)

    def move(source, target, number_of, slot, device):
        return pltpu.make_async_remote_copy(
            src_ref=source, dst_ref=target, send_sem=send_sem.at[number_of, slot],
            recv_sem=recv_sem.at[number_of, slot], device_id={"fsdp": device}, device_id_type=MESH,
        )

    column = (slice(None), y, x, c)
    hops_z = [((z + k) % depth, (z + depth - k) % depth) for k in range(1, depth)]
    small = []

    def begin(copies):
        for copy in copies:
            copy.start()
        small.extend(copies)

    def spread_z(buf, number_of):
        begin([move(buf.at[here], buf.at[here], number_of, len(PLANE) + k, number(there, y, x, c))
               for k, (there, _) in enumerate(hops_z)])

    def spread_plane(buf, number_of):
        for k, (_, source) in enumerate(hops_z):
            slot = buf.at[source, y, x, c]
            move(slot, slot, number_of, len(PLANE) + k, number(source, y, x, c)).wait_recv()
        begin([move(buf.at[column], buf.at[column], number_of, k, number(z, *peer)) for k, peer in enumerate(peers)])

    def arrived(buf, number_of):
        for k, peer in enumerate(peers):
            slot = buf.at[(slice(None),) + peer]
            move(slot, slot, number_of, k, number(z, *peer)).wait_recv()

    first, last = late[:2], late[2:]
    spread_z(power_buf, 0)
    to_plane = [move(sums.at[(slice(None),) + peer], from_plane.at[k], 2, k, number(z, *peer))
                for k, peer in enumerate(peers)]
    begin(to_plane)
    loads[0].wait()
    for part in late:
        part.start()
    advance(first)
    spread_plane(power_buf, 0)
    loads[4].wait()
    x_ref[...] = jnp.transpose(xt_ref[...].astype(jnp.float32)).astype(jnp.bfloat16)
    for copy in to_plane:
        copy.wait_recv()
    for i in range(depth):
        total = sums[i, y, x, c].astype(jnp.float32)
        for k in range(len(PLANE)):
            total = total + from_plane[k, i].astype(jnp.float32)
        z_sums[i] = total.astype(jnp.bfloat16)
    over_z = [move(z_sums.at[there], from_z.at[k], 2, len(PLANE) + k, number(there, y, x, c))
              for k, (there, _) in enumerate(hops_z)]
    begin(over_z)
    advance(last)
    arrived(power_buf, 0)

    tiles = [power_buf[d + (pl.ds(row * SUB, SUB),)] for d in devices for row in range(rows_local)]
    gram = []
    for l in range(rank):
        total = jnp.zeros((SUB, LANES), jnp.float32)
        for tile in tiles:
            total = total + tile * tile[l : l + 1]
        gram.append(total)
    lower = [[None] * rank for _ in range(rank)]
    inverse = [None] * rank
    for l in range(rank):
        value = gram[l][l : l + 1]
        for j in range(l):
            value = value - lower[l][j] * lower[l][j]
        lower[l][l] = jnp.sqrt(value)
        inverse[l] = 1.0 / lower[l][l]
        for k in range(l + 1, rank):
            value = gram[l][k : k + 1]
            for j in range(l):
                value = value - lower[k][j] * lower[l][j]
            lower[k][l] = value * inverse[l]

    def solve(right):
        found = []
        for k in range(rank):
            value = right[k]
            for j in range(k):
                value = value - lower[k][j] * found[j]
            found.append(value * inverse[k])
        return found

    for copy in over_z:
        copy.wait_recv()
    total = z_sums[z].astype(jnp.float32)
    for k in range(depth - 1):
        total = total + from_z[k].astype(jnp.float32)
    coeff_buf[here] = jnp.concatenate(
        solve([total[k * unit : (k + 1) * unit] for k in range(rank)]), axis=0
    ).astype(jnp.bfloat16)
    spread_z(coeff_buf, 1)
    advance(last)

    filler = [jnp.zeros((1, LANES), jnp.float32)] * (SUB - rank)
    for i, tile in enumerate(tiles):
        found = solve([tile[k : k + 1] for k in range(rank)])
        ortho_ref[pl.ds(i * SUB, SUB)] = jnp.concatenate(found + filler, axis=0)
    for row in range(rows_local):
        tile = own_power[row]
        found = solve([tile[k : k + 1] for k in range(rank)])
        mine_ref[pl.ds(row * SUB, SUB)] = jnp.concatenate(found + filler, axis=0)

    spread_plane(coeff_buf, 1)
    advance(first)
    arrived(coeff_buf, 1)
    squares = [jnp.zeros((unit, LANES), jnp.float32) for _ in range(rank)]
    for i in range(owners):
        slot = coeff_buf[devices[i]].astype(jnp.float32)
        for k in range(rank):
            values = slot[k * unit : (k + 1) * unit]
            coeff_ref[k, pl.ds(i * unit, unit)] = values
            squares[k] = squares[k] + values * values
    squares_ref[...] = jnp.concatenate(
        [jnp.broadcast_to(jnp.sum(squares[k], keepdims=True), (1, LANES)) for k in range(rank)] + filler, axis=0
    )

    advance(last)
    advance(first)
    for part in late:
        part.from_sibling()
    for part in late:
        part.drain()
    for copy in small:
        copy.wait_send()


def apply_kernel(scale, rank, rows_local, ortho_ref, mine_ref, squares_ref, x_ref, w_hbm, coeff_ref, buffer_ref,
                 w_ref, act_hbm, nm_ref, nb_ref, nw_ref, w_all_ref, act_ref, spread, load_sem, store_sem):
    rows, groups = w_hbm.shape[:2]
    chunks = groups // CHUNK
    block = CHUNK * LANES
    inverse = [1.0 / jnp.sqrt(squares_ref[k : k + 1] + epsilon) for k in range(rank)]

    def load(i):
        at = pl.ds(pl.multiple_of(i * CHUNK, CHUNK), CHUNK)
        return pltpu.make_async_copy(w_hbm.at[:, at], w_all_ref.at[i], load_sem.at[i])

    def store(i):
        at = pl.ds(pl.multiple_of(i * block, block), block)
        return pltpu.make_async_copy(act_ref.at[i % 2], act_hbm.at[:, at], store_sem.at[i % 2])

    for i in range(chunks):
        load(i).start()

    def one_chunk(i, carry):
        at = pl.ds(pl.multiple_of(i * CHUNK, CHUNK), CHUNK)
        coeff = [coeff_ref[k, at] for k in range(rank)]
        basis = [coeff[k] * inverse[k] for k in range(rank)]
        for k in range(rank):
            nb_ref[pl.ds(i * (CHUNK * rank) + k, CHUNK, stride=rank)] = basis[k]
        scaled = [scale * basis[k] for k in range(rank)]

        def lowered(weight, ref, row):
            change = ref[pl.ds(row * SUB, 1)] * scaled[0]
            for k in range(1, rank):
                change = change + ref[pl.ds(row * SUB + k, 1)] * scaled[k]
            return weight.astype(jnp.float32) - change

        for row in range(rows_local):
            nw_ref[row, at] = lowered(w_ref[row, at], mine_ref, row).astype(jnp.bfloat16)
            feedback = mine_ref[pl.ds(row * SUB, 1)] * coeff[0]
            for k in range(1, rank):
                feedback = feedback + mine_ref[pl.ds(row * SUB + k, 1)] * coeff[k]
            nm_ref[row, at] = buffer_ref[row, at] - (1.0 - decay_rate) * feedback
        load(i).wait()
        for row in range(rows):
            spread[pl.ds(row * PITCH, CHUNK)] = lowered(w_all_ref[i, row], ortho_ref, row)

        @pl.when(i >= 2)
        def _():
            store(i - 2).wait()

        weights = jnp.concatenate(
            [spread[pl.ds(j, rows, stride=PITCH)].astype(jnp.bfloat16) for j in range(CHUNK)], axis=1
        )
        act_ref[i % 2] = jnp.dot(
            x_ref[...], weights, preferred_element_type=jnp.float32
        ).astype(jnp.bfloat16)
        store(i).start()
        return carry

    lax.fori_loop(0, chunks, one_chunk, 0)
    for i in range(max(chunks - 2, 0), chunks):
        store(i).wait()


def on_device(fsdp, tp, momentum, gradient, basis, weight, inputs):
    rows_local, width = momentum.shape
    rank = basis.shape[0]
    rows = rows_local * fsdp
    tokens = inputs.shape[0]
    depth = fsdp // 8
    assert depth * 8 == fsdp and rank <= SUB
    scale = step_size * math.sqrt(width * tp / rows)
    block = CHUNK * LANES
    padded = -(-width // block) * block
    groups = padded // LANES
    chunks = groups // CHUNK

    def dense(array):
        if padded != width:
            array = jnp.pad(array, ((0, 0), (0, padded - width)))
        return array.reshape(array.shape[0], groups, LANES)

    m, g, w = dense(momentum), dense(gradient), dense(weight)
    b = dense(basis).transpose(1, 0, 2).reshape(groups * rank, LANES)
    if tp > 1:
        buffer = decay_rate * momentum + gradient
        power = lax.psum(
            lax.dot_general(buffer, basis, (((1,), (1,)), ((), ())), precision=highest,
                            preferred_element_type=jnp.float32), "tp")
        power = jnp.pad(power, ((0, 0), (0, SUB - rank))).reshape(rows_local * SUB, 1)
        power = jnp.broadcast_to(power, (rows_local * SUB, LANES))
    else:
        power = jnp.zeros((SUB, LANES), jnp.float32)

    vmem = pl.BlockSpec(memory_space=pltpu.VMEM)
    hbm = pl.BlockSpec(memory_space=pltpu.HBM)
    anywhere = pl.BlockSpec(memory_space=pl.ANY)
    unit = SUB * -(-groups // (SUB * fsdp))
    assert groups % unit == 0
    parts = 3 + len(split_chunks(WEIGHT_PLAN, chunks))
    f32, bf16 = jnp.float32, jnp.bfloat16
    slot = (rank * unit, LANES)
    gathered, coeff, buffer, x, ortho, mine, squares = pl.pallas_call(
        functools.partial(gather_kernel, depth, rank, rows_local, unit, tp > 1),
        out_shape=(
            jax.ShapeDtypeStruct((depth, 2, 2, 2, rows_local, groups, LANES), bf16),
            jax.ShapeDtypeStruct((rank, groups, LANES), f32),
            jax.ShapeDtypeStruct((rows_local, groups, LANES), f32),
            jax.ShapeDtypeStruct((tokens, rows), bf16),
            jax.ShapeDtypeStruct((rows * SUB, LANES), f32),
            jax.ShapeDtypeStruct((rows_local * SUB, LANES), f32),
            jax.ShapeDtypeStruct((SUB, LANES), f32),
        ),
        in_specs=[hbm] * 4 + [vmem] * 2,
        out_specs=(anywhere,) + (vmem,) * 6,
        scratch_shapes=[
            pltpu.VMEM(m.shape, f32),
            pltpu.VMEM(g.shape, f32),
            pltpu.VMEM(b.shape, f32),
            pltpu.VMEM((rows, tokens), bf16),
            pltpu.VMEM((depth, 2, 2, 2) + slot, bf16),
            pltpu.VMEM((len(PLANE), depth) + slot, bf16),
            pltpu.VMEM((depth,) + slot, bf16),
            pltpu.VMEM((depth,) + slot, bf16),
            pltpu.VMEM((depth, 2, 2, 2) + slot, bf16),
            pltpu.VMEM((depth, 2, 2, 2, rows_local * SUB, LANES), f32),
            pltpu.SemaphoreType.DMA((parts, len(PLANE) + depth)),
            pltpu.SemaphoreType.DMA((parts, len(PLANE) + depth)),
            pltpu.SemaphoreType.DMA((5,)),
        ],
        compiler_params=pltpu.CompilerParams(
            collective_id=0, has_side_effects=True, vmem_limit_bytes=63 * 1024 * 1024
        ),
        name="gather_rows",
    )(m, g, b, inputs.T, w, power)

    if tp > 1:
        squares = lax.psum(squares, "tp")
    w_all = gathered.reshape(rows, groups, LANES)

    act, nm, nb, nw = pl.pallas_call(
        functools.partial(apply_kernel, scale, rank, rows_local),
        out_shape=(
            jax.ShapeDtypeStruct((tokens, padded), bf16),
            jax.ShapeDtypeStruct((rows_local, groups, LANES), f32),
            jax.ShapeDtypeStruct((groups * rank, LANES), f32),
            jax.ShapeDtypeStruct((rows_local, groups, LANES), bf16),
        ),
        in_specs=[vmem] * 4 + [anywhere] + [vmem] * 3,
        out_specs=(anywhere, vmem, vmem, vmem),
        scratch_shapes=[
            pltpu.VMEM((chunks, rows, CHUNK, LANES), bf16),
            pltpu.VMEM((2, tokens, block), bf16),
            pltpu.VMEM((rows * PITCH, LANES), f32),
            pltpu.SemaphoreType.DMA((chunks,)),
            pltpu.SemaphoreType.DMA((2,)),
        ],
        compiler_params=pltpu.CompilerParams(vmem_limit_bytes=63 * 1024 * 1024),
        name="apply_update",
    )(ortho, mine, squares, x, w_all, coeff, buffer, w)

    def flat(array):
        return array.reshape(array.shape[0], padded)[:, :width]

    new_basis = flat(nb.reshape(groups, rank, LANES).transpose(1, 0, 2))
    return flat(nm), new_basis, flat(nw), act[:, :width]


def solution(mesh):
    return jax.shard_map(
        functools.partial(on_device, mesh.shape["fsdp"], mesh.shape["tp"]),
        mesh=mesh,
        in_specs=(
            P("fsdp", "tp"),
            P("fsdp", "tp"),
            P(None, "tp"),
            P("fsdp", "tp"),
            P("fsdp", None),
        ),
        out_specs=(P("fsdp", "tp"), P(None, "tp"), P("fsdp", "tp"), P("fsdp", "tp")),
        check_vma=False,
    )
```

```python
import functools
import math

import jax
import jax.numpy as jnp
from jax import lax
from jax.experimental import pallas as pl
from jax.experimental.pallas import tpu as pltpu
from jax.sharding import PartitionSpec as P

decay_rate = 0.8
step_size = 0.5
epsilon = 1e-06
highest = lax.Precision.HIGHEST
MESH = pl.DeviceIdType.MESH
LANES = 128
PLANE = [(y, x, c) for y in range(2) for x in range(2) for c in range(2)][1:]
CHUNK = 16
PITCH = 24
SUB = 8

WEIGHT_PLAN = (("yzx", 3), ("xzy", 3), ("zxy", 4), ("zyx", 3))


def split_chunks(plan, chunks):
    total = sum(share for _, share in plan)
    parts, start, seen = [], 0, 0
    for order, share in plan:
        seen += share
        stop = (chunks * seen) // total
        if stop > start:
            parts.append((order, start, stop - start))
        start = stop
    return parts


class Mover:
    def __init__(self, buf, window, order, number, coords, depth, send_sem, recv_sem):
        self.buf, self.window, self.order, self.number = buf, window, order, number
        self.coords, self.depth = coords, depth
        self.send_sem, self.recv_sem = send_sem, recv_sem
        self.sent = []
        self.phase = 0

    def block(self, **fixed):
        done = self.order[: self.phase]
        index = []
        for axis in "zyxc":
            if axis in fixed:
                index.append(fixed[axis])
            elif axis in done:
                index.append(slice(None))
            else:
                index.append(self.coords[axis])
        return self.buf.at[tuple(index) + self.window]

    def copy(self, ref, slot, **target):
        where = dict(self.coords, **target)
        device = ((where["z"] * 2 + where["y"]) * 2 + where["x"]) * 2 + where["c"]
        return pltpu.make_async_remote_copy(
            src_ref=ref,
            dst_ref=ref,
            send_sem=self.send_sem.at[self.number, slot],
            recv_sem=self.recv_sem.at[self.number, slot],
            device_id={"fsdp": device},
            device_id_type=MESH,
        )

    def hops(self):
        axis = self.order[self.phase]
        base = self.order.index(axis) if axis != "z" else 4
        if axis == "z":
            return [(4 + k, (self.coords["z"] + k) % self.depth, (self.coords["z"] + self.depth - k) % self.depth)
                    for k in range(1, self.depth)]
        other = 1 - self.coords[axis]
        return [(base if base < 2 else 2, other, other)]

    def start(self):
        axis = self.order[self.phase]
        for slot, target, _ in self.hops():
            copy = self.copy(self.block(), slot, **{axis: target})
            copy.start()
            self.sent.append(copy)

    def finish(self):
        axis = self.order[self.phase]
        for slot, _, source in self.hops():
            self.copy(self.block(**{axis: source}), slot, **{axis: source}).wait_recv()
        self.phase += 1

    def to_sibling(self, last):
        axis = self.order[2]
        side = 1 - self.coords[axis] if last else self.coords[axis]
        copy = self.copy(self.block(**{axis: side}), 3 if last else 4, c=1 - self.coords["c"])
        copy.start()
        self.sent.append(copy)

    def from_sibling(self):
        axis, other = self.order[2], 1 - self.coords["c"]
        for side, slot in ((self.coords[axis], 4), (1 - self.coords[axis], 3)):
            self.copy(self.block(**{axis: side, "c": other}), slot, c=other).wait_recv()

    def drain(self):
        for copy in self.sent:
            copy.wait_send()


def gather_kernel(depth, rank, rows_local, unit, has_power, *refs):
    (m_hbm, g_hbm, basis_hbm, xt_hbm, w_ref, power_ref, wide_hbm, coeff_ref, buffer_ref, x_ref, ortho_ref, mine_ref,
     squares_ref, gathered, wide, spread, m_ref, g_ref, basis_ref, xt_ref, sums, from_plane, z_sums, from_z, coeff_buf, power_buf,
     send_sem, recv_sem, local_sem, wide_sem) = refs
    groups = m_ref.shape[1]
    chunks = groups // CHUNK
    me = lax.axis_index("fsdp")
    coords = {"z": me // 8, "y": (me // 4) % 2, "x": (me // 2) % 2, "c": me % 2}
    here = (coords["z"], coords["y"], coords["x"], coords["c"])

    def number(z, y, x, c):
        return ((z * 2 + y) * 2 + x) * 2 + c

    z, y, x, c = here
    peers = [((y + dy) % 2, (x + dx) % 2, (c + dc) % 2) for dy, dx, dc in PLANE]
    partners = [number((z + k) % depth, y, x, c) for k in range(1, depth)]
    partners += [number(z, *peer) for peer in peers]
    barrier = pltpu.get_barrier_semaphore()
    for partner in partners:
        pl.semaphore_signal(barrier, inc=1, device_id={"fsdp": partner}, device_id_type=MESH)

    loads = [
        pltpu.make_async_copy(source, target, local_sem.at[i])
        for i, (source, target) in enumerate(
            ((m_hbm, m_ref), (g_hbm, g_ref), (basis_hbm, basis_ref), (xt_hbm, xt_ref))
        )
    ]
    for load in loads:
        load.start()
    gathered[here] = w_ref[...]

    def mover(buf, window, order, count):
        return Mover(buf, window, order, count, coords, depth, send_sem, recv_sem)

    late = []
    pieces = split_chunks(WEIGHT_PLAN, chunks)
    for order, start, count in pieces:
        window = (slice(None), pl.ds(start * CHUNK, count * CHUNK), slice(None))
        late.append(mover(gathered, window, order, 3 + len(late)))

    pl.semaphore_wait(barrier, len(partners))
    for part in late:
        part.start()
    for load in loads[:3]:
        load.wait()

    for row in range(rows_local):
        buffer_ref[row] = decay_rate * m_ref[row] + g_ref[row]
        if has_power:
            power_buf[here + (pl.ds(row * SUB, SUB),)] = power_ref[pl.ds(row * SUB, SUB)]
        else:
            tile = [
                jnp.broadcast_to(
                    jnp.sum(buffer_ref[row] * basis_ref[pl.ds(k, groups, stride=rank)], keepdims=True), (1, LANES)
                )
                for k in range(rank)
            ]
            tile += [jnp.zeros((1, LANES), jnp.float32)] * (SUB - rank)
            power_buf[here + (pl.ds(row * SUB, SUB),)] = jnp.concatenate(tile, axis=0)

    devices = [(z, y, x, c) for z in range(depth) for y in range(2) for x in range(2) for c in range(2)]
    owners = groups // unit
    own_power = [power_buf[here + (pl.ds(row * SUB, SUB),)] for row in range(rows_local)]
    for i, d in enumerate(devices):
        if i >= owners:
            sums[d] = jnp.zeros((rank * unit, LANES), jnp.float32)
            continue
        terms = []
        for k in range(rank):
            term = jnp.zeros((unit, LANES), jnp.float32)
            for row in range(rows_local):
                term = term + own_power[row][k : k + 1] * buffer_ref[row, pl.ds(i * unit, unit)]
            terms.append(term)
        sums[d] = jnp.concatenate(terms, axis=0)

    def advance(movers):
        for part in movers:
            part.finish()
            if part.phase == 2:
                part.to_sibling(False)
            if part.phase < 3:
                part.start()
            else:
                part.to_sibling(True)

    def move(source, target, number_of, slot, device):
        return pltpu.make_async_remote_copy(
            src_ref=source, dst_ref=target, send_sem=send_sem.at[number_of, slot],
            recv_sem=recv_sem.at[number_of, slot], device_id={"fsdp": device}, device_id_type=MESH,
        )

    column = (slice(None), y, x, c)
    hops_z = [((z + k) % depth, (z + depth - k) % depth) for k in range(1, depth)]
    small = []

    def begin(copies):
        for copy in copies:
            copy.start()
        small.extend(copies)

    def spread_z(buf, number_of):
        begin([move(buf.at[here], buf.at[here], number_of, len(PLANE) + k, number(there, y, x, c))
               for k, (there, _) in enumerate(hops_z)])

    def spread_plane(buf, number_of):
        for k, (_, source) in enumerate(hops_z):
            slot = buf.at[source, y, x, c]
            move(slot, slot, number_of, len(PLANE) + k, number(source, y, x, c)).wait_recv()
        begin([move(buf.at[column], buf.at[column], number_of, k, number(z, *peer)) for k, peer in enumerate(peers)])

    def arrived(buf, number_of):
        for k, peer in enumerate(peers):
            slot = buf.at[(slice(None),) + peer]
            move(slot, slot, number_of, k, number(z, *peer)).wait_recv()

    first, last = late[:2], late[2:]
    spread_z(power_buf, 0)
    to_plane = [move(sums.at[(slice(None),) + peer], from_plane.at[k], 2, k, number(z, *peer))
                for k, peer in enumerate(peers)]
    begin(to_plane)
    advance(first)
    spread_plane(power_buf, 0)
    loads[3].wait()
    x_ref[...] = jnp.transpose(xt_ref[...].astype(jnp.float32)).astype(jnp.bfloat16)
    for copy in to_plane:
        copy.wait_recv()
    for i in range(depth):
        total = sums[i, y, x, c]
        for k in range(len(PLANE)):
            total = total + from_plane[k, i]
        z_sums[i] = total
    over_z = [move(z_sums.at[there], from_z.at[k], 2, len(PLANE) + k, number(there, y, x, c))
              for k, (there, _) in enumerate(hops_z)]
    begin(over_z)
    advance(last)
    arrived(power_buf, 0)

    tiles = [power_buf[d + (pl.ds(row * SUB, SUB),)] for d in devices for row in range(rows_local)]
    gram = []
    for l in range(rank):
        total = jnp.zeros((SUB, LANES), jnp.float32)
        for tile in tiles:
            total = total + tile * tile[l : l + 1]
        gram.append(total)
    lower = [[None] * rank for _ in range(rank)]
    inverse = [None] * rank
    for l in range(rank):
        value = gram[l][l : l + 1]
        for j in range(l):
            value = value - lower[l][j] * lower[l][j]
        lower[l][l] = jnp.sqrt(value)
        inverse[l] = 1.0 / lower[l][l]
        for k in range(l + 1, rank):
            value = gram[l][k : k + 1]
            for j in range(l):
                value = value - lower[k][j] * lower[l][j]
            lower[k][l] = value * inverse[l]

    def solve(right):
        found = []
        for k in range(rank):
            value = right[k]
            for j in range(k):
                value = value - lower[k][j] * found[j]
            found.append(value * inverse[k])
        return found

    for copy in over_z:
        copy.wait_recv()
    total = z_sums[z]
    for k in range(depth - 1):
        total = total + from_z[k]
    coeff_buf[here] = jnp.concatenate(
        solve([total[k * unit : (k + 1) * unit] for k in range(rank)]), axis=0
    ).astype(jnp.bfloat16)
    spread_z(coeff_buf, 1)
    advance(last)

    filler = [jnp.zeros((1, LANES), jnp.float32)] * (SUB - rank)
    for i, tile in enumerate(tiles):
        found = solve([tile[k : k + 1] for k in range(rank)])
        ortho_ref[pl.ds(i * SUB, SUB)] = jnp.concatenate(found + filler, axis=0)
    for row in range(rows_local):
        tile = own_power[row]
        found = solve([tile[k : k + 1] for k in range(rank)])
        mine_ref[pl.ds(row * SUB, SUB)] = jnp.concatenate(found + filler, axis=0)

    spread_plane(coeff_buf, 1)
    advance(first)
    arrived(coeff_buf, 1)
    squares = [jnp.zeros((unit, LANES), jnp.float32) for _ in range(rank)]
    for i in range(owners):
        slot = coeff_buf[devices[i]].astype(jnp.float32)
        for k in range(rank):
            values = slot[k * unit : (k + 1) * unit]
            coeff_ref[k, pl.ds(i * unit, unit)] = values
            squares[k] = squares[k] + values * values
    squares_ref[...] = jnp.concatenate(
        [jnp.broadcast_to(jnp.sum(squares[k], keepdims=True), (1, LANES)) for k in range(rank)] + filler, axis=0
    )

    advance(last)

    rows = len(devices) * rows_local

    def relay(number):
        part, (_, start, count) = late[number], pieces[number]
        part.from_sibling()

        def one_chunk(i, carry):
            at = pl.ds(pl.multiple_of(i * CHUNK, CHUNK), CHUNK)
            for place, d in enumerate(devices):
                for row in range(rows_local):
                    spread[pl.ds((place * rows_local + row) * PITCH, CHUNK)] = gathered[d + (row, at)].astype(
                        jnp.float32
                    )
            for j in range(CHUNK):
                wide[i, pl.ds(j * rows, rows)] = spread[pl.ds(j, rows, stride=PITCH)].astype(jnp.bfloat16)
            return carry

        lax.fori_loop(start, start + count, one_chunk, 0)
        copy = pltpu.make_async_copy(
            wide.at[pl.ds(start, count)], wide_hbm.at[pl.ds(start, count)], wide_sem.at[number]
        )
        copy.start()
        return copy

    copies = []
    if len(late) <= 2:
        advance(first)
    for number in range(2, len(late)):
        copies.append(relay(number))
        if number == 2:
            advance(first)
    for number in range(min(2, len(late))):
        copies.append(relay(number))
    for copy in copies:
        copy.wait()
    for part in late:
        part.drain()
    for copy in small:
        copy.wait_send()


def apply_kernel(scale, rank, rows_local, ortho_ref, mine_ref, squares_ref, x_ref, wide_hbm, coeff_ref, buffer_ref,
                 w_ref, act_hbm, nm_ref, nb_ref, nw_ref, wide, act_ref, load_sem, store_sem):
    chunks = wide_hbm.shape[0]
    rows = wide_hbm.shape[1] // CHUNK
    block = CHUNK * LANES
    ortho = [ortho_ref[pl.ds(k, rows, stride=SUB)] for k in range(rank)]
    inverse = [1.0 / jnp.sqrt(squares_ref[k : k + 1] + epsilon) for k in range(rank)]

    def load(i):
        return pltpu.make_async_copy(wide_hbm.at[i], wide.at[i], load_sem.at[i])

    def store(i):
        at = pl.ds(pl.multiple_of(i * block, block), block)
        return pltpu.make_async_copy(act_ref.at[i % 2], act_hbm.at[:, at], store_sem.at[i % 2])

    for i in range(chunks):
        load(i).start()

    def one_chunk(i, carry):
        at = pl.ds(pl.multiple_of(i * CHUNK, CHUNK), CHUNK)
        coeff = [coeff_ref[k, at] for k in range(rank)]
        basis = [coeff[k] * inverse[k] for k in range(rank)]
        for k in range(rank):
            nb_ref[pl.ds(i * (CHUNK * rank) + k, CHUNK, stride=rank)] = basis[k]
        scaled = [scale * basis[k] for k in range(rank)]

        def lowered(weight, ref, row):
            change = ref[pl.ds(row * SUB, 1)] * scaled[0]
            for k in range(1, rank):
                change = change + ref[pl.ds(row * SUB + k, 1)] * scaled[k]
            return weight.astype(jnp.float32) - change

        for row in range(rows_local):
            nw_ref[row, at] = lowered(w_ref[row, at], mine_ref, row).astype(jnp.bfloat16)
            feedback = mine_ref[pl.ds(row * SUB, 1)] * coeff[0]
            for k in range(1, rank):
                feedback = feedback + mine_ref[pl.ds(row * SUB + k, 1)] * coeff[k]
            nm_ref[row, at] = buffer_ref[row, at] - (1.0 - decay_rate) * feedback
        load(i).wait()
        tiles = []
        for j in range(CHUNK):
            change = ortho[0] * scaled[0][j : j + 1]
            for k in range(1, rank):
                change = change + ortho[k] * scaled[k][j : j + 1]
            tile = wide[i, pl.ds(j * rows, rows)].astype(jnp.float32) - change
            tiles.append(tile.astype(jnp.bfloat16))

        @pl.when(i >= 2)
        def _():
            store(i - 2).wait()

        weights = jnp.concatenate(tiles, axis=1)
        act_ref[i % 2] = jnp.dot(
            x_ref[...], weights, preferred_element_type=jnp.float32
        ).astype(jnp.bfloat16)
        store(i).start()
        return carry

    lax.fori_loop(0, chunks, one_chunk, 0)
    for i in range(max(chunks - 2, 0), chunks):
        store(i).wait()


def on_device(fsdp, tp, momentum, gradient, basis, weight, inputs):
    rows_local, width = momentum.shape
    rank = basis.shape[0]
    rows = rows_local * fsdp
    tokens = inputs.shape[0]
    depth = fsdp // 8
    assert depth * 8 == fsdp and rank <= SUB
    scale = step_size * math.sqrt(width * tp / rows)
    block = CHUNK * LANES
    padded = -(-width // block) * block
    groups = padded // LANES
    chunks = groups // CHUNK

    def dense(array):
        if padded != width:
            array = jnp.pad(array, ((0, 0), (0, padded - width)))
        return array.reshape(array.shape[0], groups, LANES)

    m, g, w = dense(momentum), dense(gradient), dense(weight)
    b = dense(basis).transpose(1, 0, 2).reshape(groups * rank, LANES)
    if tp > 1:
        buffer = decay_rate * momentum + gradient
        power = lax.psum(
            lax.dot_general(buffer, basis, (((1,), (1,)), ((), ())), precision=highest,
                            preferred_element_type=jnp.float32), "tp")
        power = jnp.pad(power, ((0, 0), (0, SUB - rank))).reshape(rows_local * SUB, 1)
        power = jnp.broadcast_to(power, (rows_local * SUB, LANES))
    else:
        power = inputs.T

    vmem = pl.BlockSpec(memory_space=pltpu.VMEM)
    hbm = pl.BlockSpec(memory_space=pltpu.HBM)
    anywhere = pl.BlockSpec(memory_space=pl.ANY)
    unit = SUB * -(-groups // (SUB * fsdp))
    assert groups % unit == 0
    parts = 3 + len(split_chunks(WEIGHT_PLAN, chunks))
    f32, bf16 = jnp.float32, jnp.bfloat16
    slot = (rank * unit, LANES)
    wide, coeff, buffer, x, ortho, mine, squares = pl.pallas_call(
        functools.partial(gather_kernel, depth, rank, rows_local, unit, tp > 1),
        out_shape=(
            jax.ShapeDtypeStruct((chunks, CHUNK * rows, LANES), bf16),
            jax.ShapeDtypeStruct((rank, groups, LANES), f32),
            jax.ShapeDtypeStruct((rows_local, groups, LANES), f32),
            jax.ShapeDtypeStruct((tokens, rows), bf16),
            jax.ShapeDtypeStruct((rows * SUB, LANES), f32),
            jax.ShapeDtypeStruct((rows_local * SUB, LANES), f32),
            jax.ShapeDtypeStruct((SUB, LANES), f32),
        ),
        in_specs=[hbm] * 4 + [vmem, vmem if tp > 1 else hbm],
        out_specs=(anywhere,) + (vmem,) * 6,
        scratch_shapes=[
            pltpu.VMEM((depth, 2, 2, 2, rows_local, groups, LANES), bf16),
            pltpu.VMEM((chunks, CHUNK * rows, LANES), bf16),
            pltpu.VMEM((rows * PITCH, LANES), f32),
            pltpu.VMEM(m.shape, f32),
            pltpu.VMEM(g.shape, f32),
            pltpu.VMEM(b.shape, f32),
            pltpu.VMEM((rows, tokens), bf16),
            pltpu.VMEM((depth, 2, 2, 2) + slot, f32),
            pltpu.VMEM((len(PLANE), depth) + slot, f32),
            pltpu.VMEM((depth,) + slot, f32),
            pltpu.VMEM((depth,) + slot, f32),
            pltpu.VMEM((depth, 2, 2, 2) + slot, bf16),
            pltpu.VMEM((depth, 2, 2, 2, rows_local * SUB, LANES), f32),
            pltpu.SemaphoreType.DMA((parts, len(PLANE) + depth)),
            pltpu.SemaphoreType.DMA((parts, len(PLANE) + depth)),
            pltpu.SemaphoreType.DMA((4,)),
            pltpu.SemaphoreType.DMA((parts,)),
        ],
        compiler_params=pltpu.CompilerParams(
            collective_id=0, has_side_effects=True, vmem_limit_bytes=63 * 1024 * 1024
        ),
        name="gather_rows",
    )(m, g, b, inputs.T, w, power)

    if tp > 1:
        squares = lax.psum(squares, "tp")

    act, nm, nb, nw = pl.pallas_call(
        functools.partial(apply_kernel, scale, rank, rows_local),
        out_shape=(
            jax.ShapeDtypeStruct((tokens, padded), bf16),
            jax.ShapeDtypeStruct((rows_local, groups, LANES), f32),
            jax.ShapeDtypeStruct((groups * rank, LANES), f32),
            jax.ShapeDtypeStruct((rows_local, groups, LANES), bf16),
        ),
        in_specs=[vmem] * 4 + [anywhere] + [vmem] * 3,
        out_specs=(anywhere, vmem, vmem, vmem),
        scratch_shapes=[
            pltpu.VMEM((chunks, CHUNK * rows, LANES), bf16),
            pltpu.VMEM((2, tokens, block), bf16),
            pltpu.SemaphoreType.DMA((chunks,)),
            pltpu.SemaphoreType.DMA((2,)),
        ],
        compiler_params=pltpu.CompilerParams(vmem_limit_bytes=63 * 1024 * 1024),
        name="apply_update",
    )(ortho, mine, squares, x, wide, coeff, buffer, w)

    def flat(array):
        return array.reshape(array.shape[0], padded)[:, :width]

    new_basis = flat(nb.reshape(groups, rank, LANES).transpose(1, 0, 2))
    return flat(nm), new_basis, flat(nw), act[:, :width]


def solution(mesh):
    return jax.shard_map(
        functools.partial(on_device, mesh.shape["fsdp"], mesh.shape["tp"]),
        mesh=mesh,
        in_specs=(
            P("fsdp", "tp"),
            P("fsdp", "tp"),
            P(None, "tp"),
            P("fsdp", "tp"),
            P("fsdp", None),
        ),
        out_specs=(P("fsdp", "tp"), P(None, "tp"), P("fsdp", "tp"), P("fsdp", "tp")),
        check_vma=False,
    )
```

```python
import functools
import math

import jax
import jax.numpy as jnp
from jax import lax
from jax.experimental import pallas as pl
from jax.experimental.pallas import tpu as pltpu
from jax.sharding import PartitionSpec as P

decay_rate = 0.8
step_size = 0.5
epsilon = 1e-06
highest = lax.Precision.HIGHEST
MESH = pl.DeviceIdType.MESH
LANES = 128
PLANE = [(y, x, c) for y in range(2) for x in range(2) for c in range(2)][1:]
CHUNK = 16
PITCH = 24
SUB = 8

WEIGHT_PLAN = (("yzx", 3), ("xzy", 3), ("zxy", 4), ("zyx", 3))


def split_chunks(plan, chunks):
    total = sum(share for _, share in plan)
    parts, start, seen = [], 0, 0
    for order, share in plan:
        seen += share
        stop = (chunks * seen) // total
        if stop > start:
            parts.append((order, start, stop - start))
        start = stop
    return parts


class Mover:
    def __init__(self, buf, window, order, number, coords, depth, send_sem, recv_sem):
        self.buf, self.window, self.order, self.number = buf, window, order, number
        self.coords, self.depth = coords, depth
        self.send_sem, self.recv_sem = send_sem, recv_sem
        self.sent = []
        self.phase = 0

    def block(self, **fixed):
        done = self.order[: self.phase]
        index = []
        for axis in "zyxc":
            if axis in fixed:
                index.append(fixed[axis])
            elif axis in done:
                index.append(slice(None))
            else:
                index.append(self.coords[axis])
        return self.buf.at[tuple(index) + self.window]

    def copy(self, ref, slot, **target):
        where = dict(self.coords, **target)
        device = ((where["z"] * 2 + where["y"]) * 2 + where["x"]) * 2 + where["c"]
        return pltpu.make_async_remote_copy(
            src_ref=ref,
            dst_ref=ref,
            send_sem=self.send_sem.at[self.number, slot],
            recv_sem=self.recv_sem.at[self.number, slot],
            device_id={"fsdp": device},
            device_id_type=MESH,
        )

    def hops(self):
        axis = self.order[self.phase]
        base = self.order.index(axis) if axis != "z" else 4
        if axis == "z":
            return [(4 + k, (self.coords["z"] + k) % self.depth, (self.coords["z"] + self.depth - k) % self.depth)
                    for k in range(1, self.depth)]
        other = 1 - self.coords[axis]
        return [(base if base < 2 else 2, other, other)]

    def start(self):
        axis = self.order[self.phase]
        for slot, target, _ in self.hops():
            copy = self.copy(self.block(), slot, **{axis: target})
            copy.start()
            self.sent.append(copy)

    def finish(self):
        axis = self.order[self.phase]
        for slot, _, source in self.hops():
            self.copy(self.block(**{axis: source}), slot, **{axis: source}).wait_recv()
        self.phase += 1

    def to_sibling(self, last):
        axis = self.order[2]
        side = 1 - self.coords[axis] if last else self.coords[axis]
        copy = self.copy(self.block(**{axis: side}), 3 if last else 4, c=1 - self.coords["c"])
        copy.start()
        self.sent.append(copy)

    def from_sibling(self):
        axis, other = self.order[2], 1 - self.coords["c"]
        for side, slot in ((self.coords[axis], 4), (1 - self.coords[axis], 3)):
            self.copy(self.block(**{axis: side, "c": other}), slot, c=other).wait_recv()

    def drain(self):
        for copy in self.sent:
            copy.wait_send()


def gather_kernel(depth, rank, rows_local, unit, has_power, *refs):
    (m_hbm, g_hbm, basis_hbm, xt_hbm, w_ref, power_ref, wide_hbm, coeff_ref, buffer_ref, x_ref, ortho_ref, mine_ref,
     squares_ref, gathered, wide, spread, m_ref, g_ref, basis_ref, xt_ref, sums, from_plane, z_sums, from_z, coeff_buf, power_buf,
     send_sem, recv_sem, local_sem, wide_sem) = refs
    groups = m_ref.shape[1]
    chunks = groups // CHUNK
    me = lax.axis_index("fsdp")
    coords = {"z": me // 8, "y": (me // 4) % 2, "x": (me // 2) % 2, "c": me % 2}
    here = (coords["z"], coords["y"], coords["x"], coords["c"])

    def number(z, y, x, c):
        return ((z * 2 + y) * 2 + x) * 2 + c

    z, y, x, c = here
    peers = [((y + dy) % 2, (x + dx) % 2, (c + dc) % 2) for dy, dx, dc in PLANE]
    partners = [number((z + k) % depth, y, x, c) for k in range(1, depth)]
    partners += [number(z, *peer) for peer in peers]
    barrier = pltpu.get_barrier_semaphore()
    for partner in partners:
        pl.semaphore_signal(barrier, inc=1, device_id={"fsdp": partner}, device_id_type=MESH)

    loads = [
        pltpu.make_async_copy(source, target, local_sem.at[i])
        for i, (source, target) in enumerate(
            ((m_hbm, m_ref), (g_hbm, g_ref), (basis_hbm, basis_ref), (xt_hbm, xt_ref))
        )
    ]
    for load in loads:
        load.start()
    gathered[here] = w_ref[...]

    def mover(buf, window, order, count):
        return Mover(buf, window, order, count, coords, depth, send_sem, recv_sem)

    late = []
    pieces = split_chunks(WEIGHT_PLAN, chunks)
    for order, start, count in pieces:
        window = (slice(None), pl.ds(start * CHUNK, count * CHUNK), slice(None))
        late.append(mover(gathered, window, order, 3 + len(late)))

    pl.semaphore_wait(barrier, len(partners))
    for part in late:
        part.start()
    for load in loads[:3]:
        load.wait()

    for row in range(rows_local):
        buffer_ref[row] = decay_rate * m_ref[row] + g_ref[row]
        if has_power:
            power_buf[here + (pl.ds(row * SUB, SUB),)] = power_ref[pl.ds(row * SUB, SUB)]
        else:
            tile = [
                jnp.broadcast_to(
                    jnp.sum(buffer_ref[row] * basis_ref[pl.ds(k, groups, stride=rank)], keepdims=True), (1, LANES)
                )
                for k in range(rank)
            ]
            tile += [jnp.zeros((1, LANES), jnp.float32)] * (SUB - rank)
            power_buf[here + (pl.ds(row * SUB, SUB),)] = jnp.concatenate(tile, axis=0)

    devices = [(z, y, x, c) for z in range(depth) for y in range(2) for x in range(2) for c in range(2)]
    owners = groups // unit
    own_power = [power_buf[here + (pl.ds(row * SUB, SUB),)] for row in range(rows_local)]
    for i, d in enumerate(devices):
        if i >= owners:
            sums[d] = jnp.zeros((rank * unit, LANES), jnp.float32)
            continue
        terms = []
        for k in range(rank):
            term = jnp.zeros((unit, LANES), jnp.float32)
            for row in range(rows_local):
                term = term + own_power[row][k : k + 1] * buffer_ref[row, pl.ds(i * unit, unit)]
            terms.append(term)
        sums[d] = jnp.concatenate(terms, axis=0)

    def advance(movers):
        for part in movers:
            part.finish()
            if part.phase == 2:
                part.to_sibling(False)
            if part.phase < 3:
                part.start()
            else:
                part.to_sibling(True)

    def move(source, target, number_of, slot, device):
        return pltpu.make_async_remote_copy(
            src_ref=source, dst_ref=target, send_sem=send_sem.at[number_of, slot],
            recv_sem=recv_sem.at[number_of, slot], device_id={"fsdp": device}, device_id_type=MESH,
        )

    column = (slice(None), y, x, c)
    hops_z = [((z + k) % depth, (z + depth - k) % depth) for k in range(1, depth)]
    small = []

    def begin(copies):
        for copy in copies:
            copy.start()
        small.extend(copies)

    def spread_z(buf, number_of):
        begin([move(buf.at[here], buf.at[here], number_of, len(PLANE) + k, number(there, y, x, c))
               for k, (there, _) in enumerate(hops_z)])

    def spread_plane(buf, number_of):
        for k, (_, source) in enumerate(hops_z):
            slot = buf.at[source, y, x, c]
            move(slot, slot, number_of, len(PLANE) + k, number(source, y, x, c)).wait_recv()
        begin([move(buf.at[column], buf.at[column], number_of, k, number(z, *peer)) for k, peer in enumerate(peers)])

    def arrived(buf, number_of):
        for k, peer in enumerate(peers):
            slot = buf.at[(slice(None),) + peer]
            move(slot, slot, number_of, k, number(z, *peer)).wait_recv()

    first, last = late[:2], late[2:]
    spread_z(power_buf, 0)
    to_plane = [move(sums.at[(slice(None),) + peer], from_plane.at[k], 2, k, number(z, *peer))
                for k, peer in enumerate(peers)]
    begin(to_plane)
    advance(first)
    spread_plane(power_buf, 0)
    loads[3].wait()
    tokens = xt_ref.shape[1]
    features = jnp.transpose(xt_ref[...].astype(jnp.float32)).astype(jnp.bfloat16)
    for b in range(x_ref.shape[0] // tokens):
        shape = (xt_ref.shape[0], x_ref.shape[1])
        place = lax.broadcasted_iota(jnp.int32, shape, 1) == (
            lax.broadcasted_iota(jnp.int32, shape, 0) + b * shape[0]
        )
        x_ref[pl.ds(b * tokens, tokens)] = jnp.dot(
            features, jnp.where(place, 1.0, 0.0).astype(jnp.bfloat16), preferred_element_type=jnp.float32
        ).astype(jnp.bfloat16)
    for copy in to_plane:
        copy.wait_recv()
    for i in range(depth):
        total = sums[i, y, x, c]
        for k in range(len(PLANE)):
            total = total + from_plane[k, i]
        z_sums[i] = total
    over_z = [move(z_sums.at[there], from_z.at[k], 2, len(PLANE) + k, number(there, y, x, c))
              for k, (there, _) in enumerate(hops_z)]
    begin(over_z)
    advance(last)
    arrived(power_buf, 0)

    tiles = [power_buf[d + (pl.ds(row * SUB, SUB),)] for d in devices for row in range(rows_local)]
    gram = []
    for l in range(rank):
        total = jnp.zeros((SUB, LANES), jnp.float32)
        for tile in tiles:
            total = total + tile * tile[l : l + 1]
        gram.append(total)
    lower = [[None] * rank for _ in range(rank)]
    inverse = [None] * rank
    for l in range(rank):
        value = gram[l][l : l + 1]
        for j in range(l):
            value = value - lower[l][j] * lower[l][j]
        lower[l][l] = jnp.sqrt(value)
        inverse[l] = 1.0 / lower[l][l]
        for k in range(l + 1, rank):
            value = gram[l][k : k + 1]
            for j in range(l):
                value = value - lower[k][j] * lower[l][j]
            lower[k][l] = value * inverse[l]

    def solve(right):
        found = []
        for k in range(rank):
            value = right[k]
            for j in range(k):
                value = value - lower[k][j] * found[j]
            found.append(value * inverse[k])
        return found

    for copy in over_z:
        copy.wait_recv()
    total = z_sums[z]
    for k in range(depth - 1):
        total = total + from_z[k]
    coeff_buf[here] = jnp.concatenate(
        solve([total[k * unit : (k + 1) * unit] for k in range(rank)]), axis=0
    ).astype(jnp.bfloat16)
    spread_z(coeff_buf, 1)
    advance(last)

    filler = [jnp.zeros((1, LANES), jnp.float32)] * (SUB - rank)
    for i, tile in enumerate(tiles):
        found = solve([tile[k : k + 1] for k in range(rank)])
        ortho_ref[pl.ds(i * SUB, SUB)] = jnp.concatenate(found + filler, axis=0)
    for row in range(rows_local):
        tile = own_power[row]
        found = solve([tile[k : k + 1] for k in range(rank)])
        mine_ref[pl.ds(row * SUB, SUB)] = jnp.concatenate(found + filler, axis=0)

    spread_plane(coeff_buf, 1)
    advance(first)
    arrived(coeff_buf, 1)
    squares = [jnp.zeros((unit, LANES), jnp.float32) for _ in range(rank)]
    for i in range(owners):
        slot = coeff_buf[devices[i]].astype(jnp.float32)
        for k in range(rank):
            values = slot[k * unit : (k + 1) * unit]
            coeff_ref[k, pl.ds(i * unit, unit)] = values
            squares[k] = squares[k] + values * values
    squares_ref[...] = jnp.concatenate(
        [jnp.broadcast_to(jnp.sum(squares[k], keepdims=True), (1, LANES)) for k in range(rank)] + filler, axis=0
    )

    advance(last)

    rows = len(devices) * rows_local

    def relay(number):
        part, (_, start, count) = late[number], pieces[number]
        part.from_sibling()

        def one_chunk(i, carry):
            at = pl.ds(pl.multiple_of(i * CHUNK, CHUNK), CHUNK)
            for place, d in enumerate(devices):
                for row in range(rows_local):
                    spread[pl.ds((place * rows_local + row) * PITCH, CHUNK)] = gathered[d + (row, at)].astype(
                        jnp.float32
                    )
            for j in range(CHUNK):
                wide[i, pl.ds(j * rows, rows)] = spread[pl.ds(j, rows, stride=PITCH)].astype(jnp.bfloat16)
            return carry

        lax.fori_loop(start, start + count, one_chunk, 0)
        copy = pltpu.make_async_copy(
            wide.at[pl.ds(start, count)], wide_hbm.at[pl.ds(start, count)], wide_sem.at[number]
        )
        copy.start()
        return copy

    copies = []
    if len(late) <= 2:
        advance(first)
    for number in range(2, len(late)):
        copies.append(relay(number))
        if number == 2:
            advance(first)
    for number in range(min(2, len(late))):
        copies.append(relay(number))
    for copy in copies:
        copy.wait()
    for part in late:
        part.drain()
    for copy in small:
        copy.wait_send()


def apply_kernel(scale, rank, rows_local, ortho_ref, mine_ref, squares_ref, x_ref, wide_hbm, coeff_ref, buffer_ref,
                 w_ref, act_hbm, nm_ref, nb_ref, nw_ref, wide, act_ref, load_sem, store_sem):
    chunks = wide_hbm.shape[0]
    rows = wide_hbm.shape[1] // CHUNK
    block = CHUNK * LANES
    ortho = [ortho_ref[pl.ds(k, rows, stride=SUB)] for k in range(rank)]
    inverse = [1.0 / jnp.sqrt(squares_ref[k : k + 1] + epsilon) for k in range(rank)]

    def load(i):
        return pltpu.make_async_copy(wide_hbm.at[i], wide.at[i], load_sem.at[i])

    def store(i):
        at = pl.ds(pl.multiple_of(i * block, block), block)
        return pltpu.make_async_copy(act_ref.at[i % 2], act_hbm.at[:, at], store_sem.at[i % 2])

    for i in range(chunks):
        load(i).start()

    def one_chunk(i, carry):
        at = pl.ds(pl.multiple_of(i * CHUNK, CHUNK), CHUNK)
        coeff = [coeff_ref[k, at] for k in range(rank)]
        basis = [coeff[k] * inverse[k] for k in range(rank)]
        for k in range(rank):
            nb_ref[pl.ds(i * (CHUNK * rank) + k, CHUNK, stride=rank)] = basis[k]
        scaled = [scale * basis[k] for k in range(rank)]

        def lowered(weight, ref, row):
            change = ref[pl.ds(row * SUB, 1)] * scaled[0]
            for k in range(1, rank):
                change = change + ref[pl.ds(row * SUB + k, 1)] * scaled[k]
            return weight.astype(jnp.float32) - change

        for row in range(rows_local):
            nw_ref[row, at] = lowered(w_ref[row, at], mine_ref, row).astype(jnp.bfloat16)
            feedback = mine_ref[pl.ds(row * SUB, 1)] * coeff[0]
            for k in range(1, rank):
                feedback = feedback + mine_ref[pl.ds(row * SUB + k, 1)] * coeff[k]
            nm_ref[row, at] = buffer_ref[row, at] - (1.0 - decay_rate) * feedback
        load(i).wait()
        tiles = []
        for j in range(CHUNK):
            change = ortho[0] * scaled[0][j : j + 1]
            for k in range(1, rank):
                change = change + ortho[k] * scaled[k][j : j + 1]
            tile = wide[i, pl.ds(j * rows, rows)].astype(jnp.float32) - change
            tiles.append(tile.astype(jnp.bfloat16))

        @pl.when(i >= 2)
        def _():
            store(i - 2).wait()

        tokens = act_ref.shape[1]
        stack = x_ref.shape[0] // tokens
        pairs = [jnp.concatenate(tiles[j : j + 2], axis=1) for j in range(0, CHUNK, 2)]
        for first in range(0, len(pairs), stack):
            weights = jnp.concatenate(pairs[first : first + stack], axis=0)
            for b in range(stack):
                act_ref[i % 2, :, pl.ds((first + b) * 2 * LANES, 2 * LANES)] = jnp.dot(
                    x_ref[pl.ds(b * tokens, tokens)], weights, preferred_element_type=jnp.float32
                ).astype(jnp.bfloat16)
        store(i).start()
        return carry

    lax.fori_loop(0, chunks, one_chunk, 0)
    for i in range(max(chunks - 2, 0), chunks):
        store(i).wait()


def on_device(fsdp, tp, momentum, gradient, basis, weight, inputs):
    rows_local, width = momentum.shape
    rank = basis.shape[0]
    rows = rows_local * fsdp
    tokens = inputs.shape[0]
    depth = fsdp // 8
    assert depth * 8 == fsdp and rank <= SUB
    scale = step_size * math.sqrt(width * tp / rows)
    block = CHUNK * LANES
    padded = -(-width // block) * block
    groups = padded // LANES
    chunks = groups // CHUNK

    def dense(array):
        if padded != width:
            array = jnp.pad(array, ((0, 0), (0, padded - width)))
        return array.reshape(array.shape[0], groups, LANES)

    m, g, w = dense(momentum), dense(gradient), dense(weight)
    b = dense(basis).transpose(1, 0, 2).reshape(groups * rank, LANES)
    if tp > 1:
        buffer = decay_rate * momentum + gradient
        power = lax.psum(
            lax.dot_general(buffer, basis, (((1,), (1,)), ((), ())), precision=highest,
                            preferred_element_type=jnp.float32), "tp")
        power = jnp.pad(power, ((0, 0), (0, SUB - rank))).reshape(rows_local * SUB, 1)
        power = jnp.broadcast_to(power, (rows_local * SUB, LANES))
    else:
        power = inputs.T

    vmem = pl.BlockSpec(memory_space=pltpu.VMEM)
    hbm = pl.BlockSpec(memory_space=pltpu.HBM)
    anywhere = pl.BlockSpec(memory_space=pl.ANY)
    unit = SUB * -(-groups // (SUB * fsdp))
    assert groups % unit == 0
    parts = 3 + len(split_chunks(WEIGHT_PLAN, chunks))
    f32, bf16 = jnp.float32, jnp.bfloat16
    slot = (rank * unit, LANES)
    stack = 8
    while stack > 1 and stack * rows > 2 * LANES:
        stack //= 2
    wide, coeff, buffer, x, ortho, mine, squares = pl.pallas_call(
        functools.partial(gather_kernel, depth, rank, rows_local, unit, tp > 1),
        out_shape=(
            jax.ShapeDtypeStruct((chunks, CHUNK * rows, LANES), bf16),
            jax.ShapeDtypeStruct((rank, groups, LANES), f32),
            jax.ShapeDtypeStruct((rows_local, groups, LANES), f32),
            jax.ShapeDtypeStruct((stack * tokens, stack * rows), bf16),
            jax.ShapeDtypeStruct((rows * SUB, LANES), f32),
            jax.ShapeDtypeStruct((rows_local * SUB, LANES), f32),
            jax.ShapeDtypeStruct((SUB, LANES), f32),
        ),
        in_specs=[hbm] * 4 + [vmem, vmem if tp > 1 else hbm],
        out_specs=(anywhere,) + (vmem,) * 6,
        scratch_shapes=[
            pltpu.VMEM((depth, 2, 2, 2, rows_local, groups, LANES), bf16),
            pltpu.VMEM((chunks, CHUNK * rows, LANES), bf16),
            pltpu.VMEM((rows * PITCH, LANES), f32),
            pltpu.VMEM(m.shape, f32),
            pltpu.VMEM(g.shape, f32),
            pltpu.VMEM(b.shape, f32),
            pltpu.VMEM((rows, tokens), bf16),
            pltpu.VMEM((depth, 2, 2, 2) + slot, f32),
            pltpu.VMEM((len(PLANE), depth) + slot, f32),
            pltpu.VMEM((depth,) + slot, f32),
            pltpu.VMEM((depth,) + slot, f32),
            pltpu.VMEM((depth, 2, 2, 2) + slot, bf16),
            pltpu.VMEM((depth, 2, 2, 2, rows_local * SUB, LANES), f32),
            pltpu.SemaphoreType.DMA((parts, len(PLANE) + depth)),
            pltpu.SemaphoreType.DMA((parts, len(PLANE) + depth)),
            pltpu.SemaphoreType.DMA((4,)),
            pltpu.SemaphoreType.DMA((parts,)),
        ],
        compiler_params=pltpu.CompilerParams(
            collective_id=0, has_side_effects=True, vmem_limit_bytes=63 * 1024 * 1024
        ),
        name="gather_rows",
    )(m, g, b, inputs.T, w, power)

    if tp > 1:
        squares = lax.psum(squares, "tp")

    act, nm, nb, nw = pl.pallas_call(
        functools.partial(apply_kernel, scale, rank, rows_local),
        out_shape=(
            jax.ShapeDtypeStruct((tokens, padded), bf16),
            jax.ShapeDtypeStruct((rows_local, groups, LANES), f32),
            jax.ShapeDtypeStruct((groups * rank, LANES), f32),
            jax.ShapeDtypeStruct((rows_local, groups, LANES), bf16),
        ),
        in_specs=[vmem] * 4 + [anywhere] + [vmem] * 3,
        out_specs=(anywhere, vmem, vmem, vmem),
        scratch_shapes=[
            pltpu.VMEM((chunks, CHUNK * rows, LANES), bf16),
            pltpu.VMEM((2, tokens, block), bf16),
            pltpu.SemaphoreType.DMA((chunks,)),
            pltpu.SemaphoreType.DMA((2,)),
        ],
        compiler_params=pltpu.CompilerParams(vmem_limit_bytes=63 * 1024 * 1024),
        name="apply_update",
    )(ortho, mine, squares, x, wide, coeff, buffer, w)

    def flat(array):
        return array.reshape(array.shape[0], padded)[:, :width]

    new_basis = flat(nb.reshape(groups, rank, LANES).transpose(1, 0, 2))
    return flat(nm), new_basis, flat(nw), act[:, :width]


def solution(mesh):
    return jax.shard_map(
        functools.partial(on_device, mesh.shape["fsdp"], mesh.shape["tp"]),
        mesh=mesh,
        in_specs=(
            P("fsdp", "tp"),
            P("fsdp", "tp"),
            P(None, "tp"),
            P("fsdp", "tp"),
            P("fsdp", None),
        ),
        out_specs=(P("fsdp", "tp"), P(None, "tp"), P("fsdp", "tp"), P("fsdp", "tp")),
        check_vma=False,
    )
```

```python
import functools
import math

import jax
import jax.numpy as jnp
from jax import lax
from jax.experimental import pallas as pl
from jax.experimental.pallas import tpu as pltpu
from jax.sharding import PartitionSpec as P

decay_rate = 0.8
step_size = 0.5
epsilon = 1e-06
highest = lax.Precision.HIGHEST
MESH = pl.DeviceIdType.MESH
LANES = 128
PLANE = [(y, x, c) for y in range(2) for x in range(2) for c in range(2)][1:]
CHUNK = 16
STORES = 4
PITCH = 24
SUB = 8

WEIGHT_PLAN = (("yzx", 3), ("xzy", 3), ("zxy", 4), ("zyx", 3))


def split_chunks(plan, chunks):
    total = sum(share for _, share in plan)
    parts, start, seen = [], 0, 0
    for order, share in plan:
        seen += share
        stop = (chunks * seen) // total
        if stop > start:
            parts.append((order, start, stop - start))
        start = stop
    return parts


class Mover:
    def __init__(self, buf, window, order, number, coords, depth, send_sem, recv_sem):
        self.buf, self.window, self.order, self.number = buf, window, order, number
        self.coords, self.depth = coords, depth
        self.send_sem, self.recv_sem = send_sem, recv_sem
        self.sent = []
        self.phase = 0

    def block(self, **fixed):
        done = self.order[: self.phase]
        index = []
        for axis in "zyxc":
            if axis in fixed:
                index.append(fixed[axis])
            elif axis in done:
                index.append(slice(None))
            else:
                index.append(self.coords[axis])
        return self.buf.at[tuple(index) + self.window]

    def copy(self, ref, slot, **target):
        where = dict(self.coords, **target)
        device = ((where["z"] * 2 + where["y"]) * 2 + where["x"]) * 2 + where["c"]
        return pltpu.make_async_remote_copy(
            src_ref=ref,
            dst_ref=ref,
            send_sem=self.send_sem.at[self.number, slot],
            recv_sem=self.recv_sem.at[self.number, slot],
            device_id={"fsdp": device},
            device_id_type=MESH,
        )

    def hops(self):
        axis = self.order[self.phase]
        base = self.order.index(axis) if axis != "z" else 4
        if axis == "z":
            return [(4 + k, (self.coords["z"] + k) % self.depth, (self.coords["z"] + self.depth - k) % self.depth)
                    for k in range(1, self.depth)]
        other = 1 - self.coords[axis]
        return [(base if base < 2 else 2, other, other)]

    def start(self):
        axis = self.order[self.phase]
        for slot, target, _ in self.hops():
            copy = self.copy(self.block(), slot, **{axis: target})
            copy.start()
            self.sent.append(copy)

    def finish(self):
        axis = self.order[self.phase]
        for slot, _, source in self.hops():
            self.copy(self.block(**{axis: source}), slot, **{axis: source}).wait_recv()
        self.phase += 1

    def to_sibling(self, last):
        axis = self.order[2]
        side = 1 - self.coords[axis] if last else self.coords[axis]
        copy = self.copy(self.block(**{axis: side}), 3 if last else 4, c=1 - self.coords["c"])
        copy.start()
        self.sent.append(copy)

    def from_sibling(self):
        axis, other = self.order[2], 1 - self.coords["c"]
        for side, slot in ((self.coords[axis], 4), (1 - self.coords[axis], 3)):
            self.copy(self.block(**{axis: side, "c": other}), slot, c=other).wait_recv()

    def drain(self):
        for copy in self.sent:
            copy.wait_send()


def gather_kernel(depth, rank, rows_local, unit, has_power, *refs):
    (m_hbm, g_hbm, basis_hbm, xt_hbm, w_ref, power_ref, wide_hbm, coeff_ref, buffer_ref, x_ref, ortho_ref, mine_ref,
     squares_ref, gathered, wide, spread, m_ref, g_ref, basis_ref, xt_ref, sums, from_plane, z_sums, from_z, coeff_buf, power_buf,
     send_sem, recv_sem, local_sem, wide_sem) = refs
    groups = m_ref.shape[1]
    chunks = groups // CHUNK
    me = lax.axis_index("fsdp")
    coords = {"z": me // 8, "y": (me // 4) % 2, "x": (me // 2) % 2, "c": me % 2}
    here = (coords["z"], coords["y"], coords["x"], coords["c"])

    def number(z, y, x, c):
        return ((z * 2 + y) * 2 + x) * 2 + c

    z, y, x, c = here
    peers = [((y + dy) % 2, (x + dx) % 2, (c + dc) % 2) for dy, dx, dc in PLANE]
    partners = [number((z + k) % depth, y, x, c) for k in range(1, depth)]
    partners += [number(z, *peer) for peer in peers]
    barrier = pltpu.get_barrier_semaphore()
    for partner in partners:
        pl.semaphore_signal(barrier, inc=1, device_id={"fsdp": partner}, device_id_type=MESH)

    loads = [
        pltpu.make_async_copy(source, target, local_sem.at[i])
        for i, (source, target) in enumerate(
            ((m_hbm, m_ref), (g_hbm, g_ref), (basis_hbm, basis_ref), (xt_hbm, xt_ref))
        )
    ]
    for load in loads:
        load.start()
    gathered[here] = w_ref[...]

    def mover(buf, window, order, count):
        return Mover(buf, window, order, count, coords, depth, send_sem, recv_sem)

    late = []
    pieces = split_chunks(WEIGHT_PLAN, chunks)
    for order, start, count in pieces:
        window = (slice(None), pl.ds(start * CHUNK, count * CHUNK), slice(None))
        late.append(mover(gathered, window, order, 3 + len(late)))

    pl.semaphore_wait(barrier, len(partners))
    for part in late:
        part.start()
    for load in loads[:3]:
        load.wait()

    for row in range(rows_local):
        buffer_ref[row] = decay_rate * m_ref[row] + g_ref[row]
        if has_power:
            power_buf[here + (pl.ds(row * SUB, SUB),)] = power_ref[pl.ds(row * SUB, SUB)]
        else:
            tile = [
                jnp.broadcast_to(
                    jnp.sum(buffer_ref[row] * basis_ref[pl.ds(k, groups, stride=rank)], keepdims=True), (1, LANES)
                )
                for k in range(rank)
            ]
            tile += [jnp.zeros((1, LANES), jnp.float32)] * (SUB - rank)
            power_buf[here + (pl.ds(row * SUB, SUB),)] = jnp.concatenate(tile, axis=0)

    devices = [(z, y, x, c) for z in range(depth) for y in range(2) for x in range(2) for c in range(2)]
    owners = groups // unit
    own_power = [power_buf[here + (pl.ds(row * SUB, SUB),)] for row in range(rows_local)]
    for i, d in enumerate(devices):
        if i >= owners:
            sums[d] = jnp.zeros((rank * unit, LANES), jnp.float32)
            continue
        terms = []
        for k in range(rank):
            term = jnp.zeros((unit, LANES), jnp.float32)
            for row in range(rows_local):
                term = term + own_power[row][k : k + 1] * buffer_ref[row, pl.ds(i * unit, unit)]
            terms.append(term)
        sums[d] = jnp.concatenate(terms, axis=0)

    def advance(movers):
        for part in movers:
            part.finish()
            if part.phase == 2:
                part.to_sibling(False)
            if part.phase < 3:
                part.start()
            else:
                part.to_sibling(True)

    def move(source, target, number_of, slot, device):
        return pltpu.make_async_remote_copy(
            src_ref=source, dst_ref=target, send_sem=send_sem.at[number_of, slot],
            recv_sem=recv_sem.at[number_of, slot], device_id={"fsdp": device}, device_id_type=MESH,
        )

    column = (slice(None), y, x, c)
    hops_z = [((z + k) % depth, (z + depth - k) % depth) for k in range(1, depth)]
    small = []

    def begin(copies):
        for copy in copies:
            copy.start()
        small.extend(copies)

    def spread_z(buf, number_of):
        begin([move(buf.at[here], buf.at[here], number_of, len(PLANE) + k, number(there, y, x, c))
               for k, (there, _) in enumerate(hops_z)])

    def spread_plane(buf, number_of):
        for k, (_, source) in enumerate(hops_z):
            slot = buf.at[source, y, x, c]
            move(slot, slot, number_of, len(PLANE) + k, number(source, y, x, c)).wait_recv()
        begin([move(buf.at[column], buf.at[column], number_of, k, number(z, *peer)) for k, peer in enumerate(peers)])

    def arrived(buf, number_of):
        for k, peer in enumerate(peers):
            slot = buf.at[(slice(None),) + peer]
            move(slot, slot, number_of, k, number(z, *peer)).wait_recv()

    first, last = late[:2], late[2:]
    spread_z(power_buf, 0)
    to_plane = [move(sums.at[(slice(None),) + peer], from_plane.at[k], 2, k, number(z, *peer))
                for k, peer in enumerate(peers)]
    begin(to_plane)
    advance(first)
    spread_plane(power_buf, 0)
    loads[3].wait()
    tokens = xt_ref.shape[1]
    features = jnp.transpose(xt_ref[...].astype(jnp.float32)).astype(jnp.bfloat16)
    for b in range(x_ref.shape[0] // tokens):
        shape = (xt_ref.shape[0], x_ref.shape[1])
        place = lax.broadcasted_iota(jnp.int32, shape, 1) == (
            lax.broadcasted_iota(jnp.int32, shape, 0) + b * shape[0]
        )
        x_ref[pl.ds(b * tokens, tokens)] = jnp.dot(
            features, jnp.where(place, 1.0, 0.0).astype(jnp.bfloat16), preferred_element_type=jnp.float32
        ).astype(jnp.bfloat16)
    for copy in to_plane:
        copy.wait_recv()
    for i in range(depth):
        total = sums[i, y, x, c]
        for k in range(len(PLANE)):
            total = total + from_plane[k, i]
        z_sums[i] = total
    over_z = [move(z_sums.at[there], from_z.at[k], 2, len(PLANE) + k, number(there, y, x, c))
              for k, (there, _) in enumerate(hops_z)]
    begin(over_z)
    advance(last)
    arrived(power_buf, 0)

    tiles = [power_buf[d + (pl.ds(row * SUB, SUB),)] for d in devices for row in range(rows_local)]
    gram = []
    for l in range(rank):
        total = jnp.zeros((SUB, LANES), jnp.float32)
        for tile in tiles:
            total = total + tile * tile[l : l + 1]
        gram.append(total)
    lower = [[None] * rank for _ in range(rank)]
    inverse = [None] * rank
    for l in range(rank):
        value = gram[l][l : l + 1]
        for j in range(l):
            value = value - lower[l][j] * lower[l][j]
        lower[l][l] = jnp.sqrt(value)
        inverse[l] = 1.0 / lower[l][l]
        for k in range(l + 1, rank):
            value = gram[l][k : k + 1]
            for j in range(l):
                value = value - lower[k][j] * lower[l][j]
            lower[k][l] = value * inverse[l]

    def solve(right):
        found = []
        for k in range(rank):
            value = right[k]
            for j in range(k):
                value = value - lower[k][j] * found[j]
            found.append(value * inverse[k])
        return found

    for copy in over_z:
        copy.wait_recv()
    total = z_sums[z]
    for k in range(depth - 1):
        total = total + from_z[k]
    coeff_buf[here] = jnp.concatenate(
        solve([total[k * unit : (k + 1) * unit] for k in range(rank)]), axis=0
    ).astype(jnp.bfloat16)
    spread_z(coeff_buf, 1)
    advance(last)

    filler = [jnp.zeros((1, LANES), jnp.float32)] * (SUB - rank)
    for i, tile in enumerate(tiles):
        found = solve([tile[k : k + 1] for k in range(rank)])
        ortho_ref[pl.ds(i * SUB, SUB)] = jnp.concatenate(found + filler, axis=0)
    for row in range(rows_local):
        tile = own_power[row]
        found = solve([tile[k : k + 1] for k in range(rank)])
        mine_ref[pl.ds(row * SUB, SUB)] = jnp.concatenate(found + filler, axis=0)

    spread_plane(coeff_buf, 1)
    advance(first)
    arrived(coeff_buf, 1)
    squares = [jnp.zeros((unit, LANES), jnp.float32) for _ in range(rank)]
    for i in range(owners):
        slot = coeff_buf[devices[i]].astype(jnp.float32)
        for k in range(rank):
            values = slot[k * unit : (k + 1) * unit]
            coeff_ref[k, pl.ds(i * unit, unit)] = values
            squares[k] = squares[k] + values * values
    squares_ref[...] = jnp.concatenate(
        [jnp.broadcast_to(jnp.sum(squares[k], keepdims=True), (1, LANES)) for k in range(rank)] + filler, axis=0
    )

    advance(last)

    rows = len(devices) * rows_local

    def relay(number):
        part, (_, start, count) = late[number], pieces[number]
        part.from_sibling()

        def one_chunk(i, carry):
            at = pl.ds(pl.multiple_of(i * CHUNK, CHUNK), CHUNK)
            for place, d in enumerate(devices):
                for row in range(rows_local):
                    spread[pl.ds((place * rows_local + row) * PITCH, CHUNK)] = gathered[d + (row, at)].astype(
                        jnp.float32
                    )
            for j in range(CHUNK):
                wide[i, pl.ds(j * rows, rows)] = spread[pl.ds(j, rows, stride=PITCH)].astype(jnp.bfloat16)
            return carry

        lax.fori_loop(start, start + count, one_chunk, 0)
        copy = pltpu.make_async_copy(
            wide.at[pl.ds(start, count)], wide_hbm.at[pl.ds(start, count)], wide_sem.at[number]
        )
        copy.start()
        return copy

    copies = []
    if len(late) <= 2:
        advance(first)
    for number in range(2, len(late)):
        copies.append(relay(number))
        if number == 2:
            advance(first)
    for number in range(min(2, len(late))):
        copies.append(relay(number))
    for copy in copies:
        copy.wait()
    for part in late:
        part.drain()
    for copy in small:
        copy.wait_send()


def apply_kernel(scale, rank, rows_local, ortho_ref, mine_ref, squares_ref, x_ref, wide_hbm, coeff_ref, buffer_ref,
                 w_ref, act_hbm, nm_ref, nb_ref, nw_ref, wide, act_ref, load_sem, store_sem):
    chunks = wide_hbm.shape[0]
    rows = wide_hbm.shape[1] // CHUNK
    block = CHUNK * LANES
    ortho = [ortho_ref[pl.ds(k, rows, stride=SUB)] for k in range(rank)]
    inverse = [1.0 / jnp.sqrt(squares_ref[k : k + 1] + epsilon) for k in range(rank)]

    def load(i):
        return pltpu.make_async_copy(wide_hbm.at[i], wide.at[i], load_sem.at[i])

    share = act_ref.shape[1] // STORES

    def stores(i):
        at = pl.ds(pl.multiple_of(i * block, block), block)
        return [
            pltpu.make_async_copy(
                act_ref.at[i, pl.ds(q * share, share)], act_hbm.at[pl.ds(q * share, share), at], store_sem.at[i, q]
            )
            for q in range(STORES)
        ]

    for i in range(chunks):
        load(i).start()

    def one_chunk(i, carry):
        at = pl.ds(pl.multiple_of(i * CHUNK, CHUNK), CHUNK)
        coeff = [coeff_ref[k, at] for k in range(rank)]
        basis = [coeff[k] * inverse[k] for k in range(rank)]
        for k in range(rank):
            nb_ref[pl.ds(i * (CHUNK * rank) + k, CHUNK, stride=rank)] = basis[k]
        scaled = [scale * basis[k] for k in range(rank)]

        def lowered(weight, ref, row):
            change = ref[pl.ds(row * SUB, 1)] * scaled[0]
            for k in range(1, rank):
                change = change + ref[pl.ds(row * SUB + k, 1)] * scaled[k]
            return weight.astype(jnp.float32) - change

        for row in range(rows_local):
            nw_ref[row, at] = lowered(w_ref[row, at], mine_ref, row).astype(jnp.bfloat16)
            feedback = mine_ref[pl.ds(row * SUB, 1)] * coeff[0]
            for k in range(1, rank):
                feedback = feedback + mine_ref[pl.ds(row * SUB + k, 1)] * coeff[k]
            nm_ref[row, at] = buffer_ref[row, at] - (1.0 - decay_rate) * feedback
        load(i).wait()
        tiles = []
        for j in range(CHUNK):
            change = ortho[0] * scaled[0][j : j + 1]
            for k in range(1, rank):
                change = change + ortho[k] * scaled[k][j : j + 1]
            tile = wide[i, pl.ds(j * rows, rows)].astype(jnp.float32) - change
            tiles.append(tile.astype(jnp.bfloat16))

        tokens = act_ref.shape[1]
        stack = x_ref.shape[0] // tokens
        pairs = [jnp.concatenate(tiles[j : j + 2], axis=1) for j in range(0, CHUNK, 2)]
        for first in range(0, len(pairs), stack):
            weights = jnp.concatenate(pairs[first : first + stack], axis=0)
            for b in range(stack):
                act_ref[i, :, pl.ds((first + b) * 2 * LANES, 2 * LANES)] = jnp.dot(
                    x_ref[pl.ds(b * tokens, tokens)], weights, preferred_element_type=jnp.float32
                ).astype(jnp.bfloat16)
        for copy in stores(i):
            copy.start()
        return carry

    lax.fori_loop(0, chunks, one_chunk, 0)
    for i in range(chunks):
        for copy in stores(i):
            copy.wait()


def on_device(fsdp, tp, momentum, gradient, basis, weight, inputs):
    rows_local, width = momentum.shape
    rank = basis.shape[0]
    rows = rows_local * fsdp
    tokens = inputs.shape[0]
    depth = fsdp // 8
    assert depth * 8 == fsdp and rank <= SUB
    scale = step_size * math.sqrt(width * tp / rows)
    block = CHUNK * LANES
    padded = -(-width // block) * block
    groups = padded // LANES
    chunks = groups // CHUNK

    def dense(array):
        if padded != width:
            array = jnp.pad(array, ((0, 0), (0, padded - width)))
        return array.reshape(array.shape[0], groups, LANES)

    m, g, w = dense(momentum), dense(gradient), dense(weight)
    b = dense(basis).transpose(1, 0, 2).reshape(groups * rank, LANES)
    if tp > 1:
        buffer = decay_rate * momentum + gradient
        power = lax.psum(
            lax.dot_general(buffer, basis, (((1,), (1,)), ((), ())), precision=highest,
                            preferred_element_type=jnp.float32), "tp")
        power = jnp.pad(power, ((0, 0), (0, SUB - rank))).reshape(rows_local * SUB, 1)
        power = jnp.broadcast_to(power, (rows_local * SUB, LANES))
    else:
        power = inputs.T

    vmem = pl.BlockSpec(memory_space=pltpu.VMEM)
    hbm = pl.BlockSpec(memory_space=pltpu.HBM)
    anywhere = pl.BlockSpec(memory_space=pl.ANY)
    unit = SUB * -(-groups // (SUB * fsdp))
    assert groups % unit == 0
    parts = 3 + len(split_chunks(WEIGHT_PLAN, chunks))
    f32, bf16 = jnp.float32, jnp.bfloat16
    slot = (rank * unit, LANES)
    stack = 8
    while stack > 1 and stack * rows > 2 * LANES:
        stack //= 2
    wide, coeff, buffer, x, ortho, mine, squares = pl.pallas_call(
        functools.partial(gather_kernel, depth, rank, rows_local, unit, tp > 1),
        out_shape=(
            jax.ShapeDtypeStruct((chunks, CHUNK * rows, LANES), bf16),
            jax.ShapeDtypeStruct((rank, groups, LANES), f32),
            jax.ShapeDtypeStruct((rows_local, groups, LANES), f32),
            jax.ShapeDtypeStruct((stack * tokens, stack * rows), bf16),
            jax.ShapeDtypeStruct((rows * SUB, LANES), f32),
            jax.ShapeDtypeStruct((rows_local * SUB, LANES), f32),
            jax.ShapeDtypeStruct((SUB, LANES), f32),
        ),
        in_specs=[hbm] * 4 + [vmem, vmem if tp > 1 else hbm],
        out_specs=(anywhere,) + (vmem,) * 6,
        scratch_shapes=[
            pltpu.VMEM((depth, 2, 2, 2, rows_local, groups, LANES), bf16),
            pltpu.VMEM((chunks, CHUNK * rows, LANES), bf16),
            pltpu.VMEM((rows * PITCH, LANES), f32),
            pltpu.VMEM(m.shape, f32),
            pltpu.VMEM(g.shape, f32),
            pltpu.VMEM(b.shape, f32),
            pltpu.VMEM((rows, tokens), bf16),
            pltpu.VMEM((depth, 2, 2, 2) + slot, f32),
            pltpu.VMEM((len(PLANE), depth) + slot, f32),
            pltpu.VMEM((depth,) + slot, f32),
            pltpu.VMEM((depth,) + slot, f32),
            pltpu.VMEM((depth, 2, 2, 2) + slot, bf16),
            pltpu.VMEM((depth, 2, 2, 2, rows_local * SUB, LANES), f32),
            pltpu.SemaphoreType.DMA((parts, len(PLANE) + depth)),
            pltpu.SemaphoreType.DMA((parts, len(PLANE) + depth)),
            pltpu.SemaphoreType.DMA((4,)),
            pltpu.SemaphoreType.DMA((parts,)),
        ],
        compiler_params=pltpu.CompilerParams(
            collective_id=0, has_side_effects=True, vmem_limit_bytes=63 * 1024 * 1024
        ),
        name="gather_rows",
    )(m, g, b, inputs.T, w, power)

    if tp > 1:
        squares = lax.psum(squares, "tp")

    act, nm, nb, nw = pl.pallas_call(
        functools.partial(apply_kernel, scale, rank, rows_local),
        out_shape=(
            jax.ShapeDtypeStruct((tokens, padded), bf16),
            jax.ShapeDtypeStruct((rows_local, groups, LANES), f32),
            jax.ShapeDtypeStruct((groups * rank, LANES), f32),
            jax.ShapeDtypeStruct((rows_local, groups, LANES), bf16),
        ),
        in_specs=[vmem] * 4 + [anywhere] + [vmem] * 3,
        out_specs=(anywhere, vmem, vmem, vmem),
        scratch_shapes=[
            pltpu.VMEM((chunks, CHUNK * rows, LANES), bf16),
            pltpu.VMEM((chunks, tokens, block), bf16),
            pltpu.SemaphoreType.DMA((chunks,)),
            pltpu.SemaphoreType.DMA((chunks, STORES)),
        ],
        compiler_params=pltpu.CompilerParams(vmem_limit_bytes=63 * 1024 * 1024),
        name="apply_update",
    )(ortho, mine, squares, x, wide, coeff, buffer, w)

    def flat(array):
        return array.reshape(array.shape[0], padded)[:, :width]

    new_basis = flat(nb.reshape(groups, rank, LANES).transpose(1, 0, 2))
    return flat(nm), new_basis, flat(nw), act[:, :width]


def solution(mesh):
    return jax.shard_map(
        functools.partial(on_device, mesh.shape["fsdp"], mesh.shape["tp"]),
        mesh=mesh,
        in_specs=(
            P("fsdp", "tp"),
            P("fsdp", "tp"),
            P(None, "tp"),
            P("fsdp", "tp"),
            P("fsdp", None),
        ),
        out_specs=(P("fsdp", "tp"), P(None, "tp"), P("fsdp", "tp"), P("fsdp", "tp")),
        check_vma=False,
    )
```

```python
import functools
import math

import jax
import jax.numpy as jnp
from jax import lax
from jax.experimental import pallas as pl
from jax.experimental.pallas import tpu as pltpu
from jax.sharding import PartitionSpec as P

decay_rate = 0.8
step_size = 0.5
epsilon = 1e-06
highest = lax.Precision.HIGHEST
MESH = pl.DeviceIdType.MESH
LANES = 128
PLANE = [(y, x, c) for y in range(2) for x in range(2) for c in range(2)][1:]
CHUNK = 16
STORES = 4
PITCH = 24
SUB = 8

WEIGHT_PLAN = (("yzx", 3), ("xzy", 3), ("zxy", 4), ("zyx", 3))


def split_chunks(plan, chunks):
    total = sum(share for _, share in plan)
    parts, start, seen = [], 0, 0
    for order, share in plan:
        seen += share
        stop = (chunks * seen) // total
        if stop > start:
            parts.append((order, start, stop - start))
        start = stop
    return parts


class Mover:
    def __init__(self, buf, window, order, number, coords, depth, send_sem, recv_sem):
        self.buf, self.window, self.order, self.number = buf, window, order, number
        self.coords, self.depth = coords, depth
        self.send_sem, self.recv_sem = send_sem, recv_sem
        self.sent = []
        self.phase = 0

    def block(self, **fixed):
        done = self.order[: self.phase]
        index = []
        for axis in "zyxc":
            if axis in fixed:
                index.append(fixed[axis])
            elif axis in done:
                index.append(slice(None))
            else:
                index.append(self.coords[axis])
        return self.buf.at[tuple(index) + self.window]

    def copy(self, ref, slot, **target):
        where = dict(self.coords, **target)
        device = ((where["z"] * 2 + where["y"]) * 2 + where["x"]) * 2 + where["c"]
        return pltpu.make_async_remote_copy(
            src_ref=ref,
            dst_ref=ref,
            send_sem=self.send_sem.at[self.number, slot],
            recv_sem=self.recv_sem.at[self.number, slot],
            device_id={"fsdp": device},
            device_id_type=MESH,
        )

    def hops(self):
        axis = self.order[self.phase]
        base = self.order.index(axis) if axis != "z" else 4
        if axis == "z":
            return [(4 + k, (self.coords["z"] + k) % self.depth, (self.coords["z"] + self.depth - k) % self.depth)
                    for k in range(1, self.depth)]
        other = 1 - self.coords[axis]
        return [(base if base < 2 else 2, other, other)]

    def start(self):
        axis = self.order[self.phase]
        for slot, target, _ in self.hops():
            copy = self.copy(self.block(), slot, **{axis: target})
            copy.start()
            self.sent.append(copy)

    def finish(self):
        axis = self.order[self.phase]
        for slot, _, source in self.hops():
            self.copy(self.block(**{axis: source}), slot, **{axis: source}).wait_recv()
        self.phase += 1

    def to_sibling(self, last):
        axis = self.order[2]
        side = 1 - self.coords[axis] if last else self.coords[axis]
        copy = self.copy(self.block(**{axis: side}), 3 if last else 4, c=1 - self.coords["c"])
        copy.start()
        self.sent.append(copy)

    def from_sibling(self):
        axis, other = self.order[2], 1 - self.coords["c"]
        for side, slot in ((self.coords[axis], 4), (1 - self.coords[axis], 3)):
            self.copy(self.block(**{axis: side, "c": other}), slot, c=other).wait_recv()

    def drain(self):
        for copy in self.sent:
            copy.wait_send()


def gather_kernel(depth, rank, rows_local, unit, has_power, *refs):
    (m_hbm, g_hbm, basis_hbm, xt_hbm, w_ref, power_ref, wide_hbm, w_out, coeff_ref, buffer_ref, x_ref, ortho_ref, mine_ref,
     squares_ref, gathered, wide, spread, m_ref, g_ref, basis_ref, xt_ref, sums, from_plane, z_sums, from_z, coeff_buf, power_buf,
     send_sem, recv_sem, local_sem, wide_sem) = refs
    groups = m_ref.shape[1]
    chunks = groups // CHUNK
    me = lax.axis_index("fsdp")
    coords = {"z": me // 8, "y": (me // 4) % 2, "x": (me // 2) % 2, "c": me % 2}
    here = (coords["z"], coords["y"], coords["x"], coords["c"])

    def number(z, y, x, c):
        return ((z * 2 + y) * 2 + x) * 2 + c

    z, y, x, c = here
    peers = [((y + dy) % 2, (x + dx) % 2, (c + dc) % 2) for dy, dx, dc in PLANE]
    partners = [number((z + k) % depth, y, x, c) for k in range(1, depth)]
    partners += [number(z, *peer) for peer in peers]
    barrier = pltpu.get_barrier_semaphore()
    for partner in partners:
        pl.semaphore_signal(barrier, inc=1, device_id={"fsdp": partner}, device_id_type=MESH)

    loads = [
        pltpu.make_async_copy(source, target, local_sem.at[i])
        for i, (source, target) in enumerate(
            ((m_hbm, m_ref), (g_hbm, g_ref), (basis_hbm, basis_ref), (xt_hbm, xt_ref))
        )
    ]
    for load in loads:
        load.start()
    if len(w_ref.shape) == 3:
        w_out[...] = w_ref[...]
    else:
        for first in range(0, groups, CHUNK):
            lines = [w_ref[:, pl.ds((first + j) * LANES, LANES)].astype(jnp.float32) for j in range(CHUNK)]
            w_out[0, pl.ds(first, CHUNK)] = jnp.concatenate(lines, axis=0).astype(jnp.bfloat16)
    gathered[here] = w_out[...]

    def mover(buf, window, order, count):
        return Mover(buf, window, order, count, coords, depth, send_sem, recv_sem)

    late = []
    pieces = split_chunks(WEIGHT_PLAN, chunks)
    for order, start, count in pieces:
        window = (slice(None), pl.ds(start * CHUNK, count * CHUNK), slice(None))
        late.append(mover(gathered, window, order, 3 + len(late)))

    pl.semaphore_wait(barrier, len(partners))
    for part in late:
        part.start()
    for load in loads[:3]:
        load.wait()

    for row in range(rows_local):
        buffer_ref[row] = decay_rate * m_ref[row] + g_ref[row]
        if has_power:
            power_buf[here + (pl.ds(row * SUB, SUB),)] = power_ref[pl.ds(row * SUB, SUB)]
        else:
            tile = [
                jnp.broadcast_to(
                    jnp.sum(buffer_ref[row] * basis_ref[pl.ds(k, groups, stride=rank)], keepdims=True), (1, LANES)
                )
                for k in range(rank)
            ]
            tile += [jnp.zeros((1, LANES), jnp.float32)] * (SUB - rank)
            power_buf[here + (pl.ds(row * SUB, SUB),)] = jnp.concatenate(tile, axis=0)

    devices = [(z, y, x, c) for z in range(depth) for y in range(2) for x in range(2) for c in range(2)]
    owners = groups // unit
    own_power = [power_buf[here + (pl.ds(row * SUB, SUB),)] for row in range(rows_local)]
    for i, d in enumerate(devices):
        if i >= owners:
            sums[d] = jnp.zeros((rank * unit, LANES), jnp.float32)
            continue
        terms = []
        for k in range(rank):
            term = jnp.zeros((unit, LANES), jnp.float32)
            for row in range(rows_local):
                term = term + own_power[row][k : k + 1] * buffer_ref[row, pl.ds(i * unit, unit)]
            terms.append(term)
        sums[d] = jnp.concatenate(terms, axis=0)

    def advance(movers):
        for part in movers:
            part.finish()
            if part.phase == 2:
                part.to_sibling(False)
            if part.phase < 3:
                part.start()
            else:
                part.to_sibling(True)

    def move(source, target, number_of, slot, device):
        return pltpu.make_async_remote_copy(
            src_ref=source, dst_ref=target, send_sem=send_sem.at[number_of, slot],
            recv_sem=recv_sem.at[number_of, slot], device_id={"fsdp": device}, device_id_type=MESH,
        )

    column = (slice(None), y, x, c)
    hops_z = [((z + k) % depth, (z + depth - k) % depth) for k in range(1, depth)]
    small = []

    def begin(copies):
        for copy in copies:
            copy.start()
        small.extend(copies)

    def spread_z(buf, number_of):
        begin([move(buf.at[here], buf.at[here], number_of, len(PLANE) + k, number(there, y, x, c))
               for k, (there, _) in enumerate(hops_z)])

    def spread_plane(buf, number_of):
        for k, (_, source) in enumerate(hops_z):
            slot = buf.at[source, y, x, c]
            move(slot, slot, number_of, len(PLANE) + k, number(source, y, x, c)).wait_recv()
        begin([move(buf.at[column], buf.at[column], number_of, k, number(z, *peer)) for k, peer in enumerate(peers)])

    def arrived(buf, number_of):
        for k, peer in enumerate(peers):
            slot = buf.at[(slice(None),) + peer]
            move(slot, slot, number_of, k, number(z, *peer)).wait_recv()

    first, last = late[:2], late[2:]
    spread_z(power_buf, 0)
    to_plane = [move(sums.at[(slice(None),) + peer], from_plane.at[k], 2, k, number(z, *peer))
                for k, peer in enumerate(peers)]
    begin(to_plane)
    advance(first)
    spread_plane(power_buf, 0)
    loads[3].wait()
    tokens = xt_ref.shape[1]
    features = jnp.transpose(xt_ref[...].astype(jnp.float32)).astype(jnp.bfloat16)
    for b in range(x_ref.shape[0] // tokens):
        shape = (xt_ref.shape[0], x_ref.shape[1])
        place = lax.broadcasted_iota(jnp.int32, shape, 1) == (
            lax.broadcasted_iota(jnp.int32, shape, 0) + b * shape[0]
        )
        x_ref[pl.ds(b * tokens, tokens)] = jnp.dot(
            features, jnp.where(place, 1.0, 0.0).astype(jnp.bfloat16), preferred_element_type=jnp.float32
        ).astype(jnp.bfloat16)
    for copy in to_plane:
        copy.wait_recv()
    for i in range(depth):
        total = sums[i, y, x, c]
        for k in range(len(PLANE)):
            total = total + from_plane[k, i]
        z_sums[i] = total
    over_z = [move(z_sums.at[there], from_z.at[k], 2, len(PLANE) + k, number(there, y, x, c))
              for k, (there, _) in enumerate(hops_z)]
    begin(over_z)
    advance(last)
    arrived(power_buf, 0)

    tiles = [power_buf[d + (pl.ds(row * SUB, SUB),)] for d in devices for row in range(rows_local)]
    gram = []
    for l in range(rank):
        total = jnp.zeros((SUB, LANES), jnp.float32)
        for tile in tiles:
            total = total + tile * tile[l : l + 1]
        gram.append(total)
    lower = [[None] * rank for _ in range(rank)]
    inverse = [None] * rank
    for l in range(rank):
        value = gram[l][l : l + 1]
        for j in range(l):
            value = value - lower[l][j] * lower[l][j]
        lower[l][l] = jnp.sqrt(value)
        inverse[l] = 1.0 / lower[l][l]
        for k in range(l + 1, rank):
            value = gram[l][k : k + 1]
            for j in range(l):
                value = value - lower[k][j] * lower[l][j]
            lower[k][l] = value * inverse[l]

    def solve(right):
        found = []
        for k in range(rank):
            value = right[k]
            for j in range(k):
                value = value - lower[k][j] * found[j]
            found.append(value * inverse[k])
        return found

    for copy in over_z:
        copy.wait_recv()
    total = z_sums[z]
    for k in range(depth - 1):
        total = total + from_z[k]
    coeff_buf[here] = jnp.concatenate(
        solve([total[k * unit : (k + 1) * unit] for k in range(rank)]), axis=0
    ).astype(jnp.bfloat16)
    spread_z(coeff_buf, 1)
    advance(last)

    filler = [jnp.zeros((1, LANES), jnp.float32)] * (SUB - rank)
    for i, tile in enumerate(tiles):
        found = solve([tile[k : k + 1] for k in range(rank)])
        ortho_ref[pl.ds(i * SUB, SUB)] = jnp.concatenate(found + filler, axis=0)
    for row in range(rows_local):
        tile = own_power[row]
        found = solve([tile[k : k + 1] for k in range(rank)])
        mine_ref[pl.ds(row * SUB, SUB)] = jnp.concatenate(found + filler, axis=0)

    spread_plane(coeff_buf, 1)
    advance(first)
    arrived(coeff_buf, 1)
    squares = [jnp.zeros((unit, LANES), jnp.float32) for _ in range(rank)]
    for i in range(owners):
        slot = coeff_buf[devices[i]].astype(jnp.float32)
        for k in range(rank):
            values = slot[k * unit : (k + 1) * unit]
            coeff_ref[k, pl.ds(i * unit, unit)] = values
            squares[k] = squares[k] + values * values
    squares_ref[...] = jnp.concatenate(
        [jnp.broadcast_to(jnp.sum(squares[k], keepdims=True), (1, LANES)) for k in range(rank)] + filler, axis=0
    )

    advance(last)

    rows = len(devices) * rows_local

    def relay(number):
        part, (_, start, count) = late[number], pieces[number]
        part.from_sibling()

        def one_chunk(i, carry):
            at = pl.ds(pl.multiple_of(i * CHUNK, CHUNK), CHUNK)
            for place, d in enumerate(devices):
                for row in range(rows_local):
                    spread[pl.ds((place * rows_local + row) * PITCH, CHUNK)] = gathered[d + (row, at)].astype(
                        jnp.float32
                    )
            for j in range(CHUNK):
                wide[i, pl.ds(j * rows, rows)] = spread[pl.ds(j, rows, stride=PITCH)].astype(jnp.bfloat16)
            return carry

        lax.fori_loop(start, start + count, one_chunk, 0)
        copy = pltpu.make_async_copy(
            wide.at[pl.ds(start, count)], wide_hbm.at[pl.ds(start, count)], wide_sem.at[number]
        )
        copy.start()
        return copy

    copies = []
    if len(late) <= 2:
        advance(first)
    for number in range(2, len(late)):
        copies.append(relay(number))
        if number == 2:
            advance(first)
    for number in range(min(2, len(late))):
        copies.append(relay(number))
    for copy in copies:
        copy.wait()
    for part in late:
        part.drain()
    for copy in small:
        copy.wait_send()


def apply_kernel(scale, rank, rows_local, ortho_ref, mine_ref, squares_ref, x_ref, wide_hbm, coeff_ref, buffer_ref,
                 w_ref, act_hbm, nm_ref, nb_ref, nw_ref, wide, act_ref, load_sem, store_sem):
    chunks = wide_hbm.shape[0]
    rows = wide_hbm.shape[1] // CHUNK
    block = CHUNK * LANES
    ortho = [ortho_ref[pl.ds(k, rows, stride=SUB)] for k in range(rank)]
    inverse = [1.0 / jnp.sqrt(squares_ref[k : k + 1] + epsilon) for k in range(rank)]

    def load(i):
        return pltpu.make_async_copy(wide_hbm.at[i], wide.at[i], load_sem.at[i])

    share = act_ref.shape[1] // STORES

    def stores(i):
        at = pl.ds(pl.multiple_of(i * block, block), block)
        return [
            pltpu.make_async_copy(
                act_ref.at[i, pl.ds(q * share, share)], act_hbm.at[pl.ds(q * share, share), at], store_sem.at[i, q]
            )
            for q in range(STORES)
        ]

    for i in range(chunks):
        load(i).start()

    def one_chunk(i, carry):
        at = pl.ds(pl.multiple_of(i * CHUNK, CHUNK), CHUNK)
        coeff = [coeff_ref[k, at] for k in range(rank)]
        basis = [coeff[k] * inverse[k] for k in range(rank)]
        for k in range(rank):
            nb_ref[pl.ds(i * (CHUNK * rank) + k, CHUNK, stride=rank)] = basis[k]
        scaled = [scale * basis[k] for k in range(rank)]

        def lowered(weight, ref, row):
            change = ref[pl.ds(row * SUB, 1)] * scaled[0]
            for k in range(1, rank):
                change = change + ref[pl.ds(row * SUB + k, 1)] * scaled[k]
            return weight.astype(jnp.float32) - change

        for row in range(rows_local):
            lowered_row = lowered(w_ref[row, at], mine_ref, row)
            if len(nw_ref.shape) == 3:
                nw_ref[row, at] = lowered_row.astype(jnp.bfloat16)
            else:
                line = jnp.concatenate([lowered_row[j : j + 1] for j in range(CHUNK)], axis=1)
                nw_ref[:, pl.ds(pl.multiple_of(i * block, block), block)] = line.astype(jnp.bfloat16)
            feedback = mine_ref[pl.ds(row * SUB, 1)] * coeff[0]
            for k in range(1, rank):
                feedback = feedback + mine_ref[pl.ds(row * SUB + k, 1)] * coeff[k]
            nm_ref[row, at] = buffer_ref[row, at] - (1.0 - decay_rate) * feedback
        load(i).wait()
        tiles = []
        for j in range(CHUNK):
            change = ortho[0] * scaled[0][j : j + 1]
            for k in range(1, rank):
                change = change + ortho[k] * scaled[k][j : j + 1]
            tile = wide[i, pl.ds(j * rows, rows)].astype(jnp.float32) - change
            tiles.append(tile.astype(jnp.bfloat16))

        tokens = act_ref.shape[1]
        stack = x_ref.shape[0] // tokens
        pairs = [jnp.concatenate(tiles[j : j + 2], axis=1) for j in range(0, CHUNK, 2)]
        for first in range(0, len(pairs), stack):
            weights = jnp.concatenate(pairs[first : first + stack], axis=0)
            for b in range(stack):
                act_ref[i, :, pl.ds((first + b) * 2 * LANES, 2 * LANES)] = jnp.dot(
                    x_ref[pl.ds(b * tokens, tokens)], weights, preferred_element_type=jnp.float32
                ).astype(jnp.bfloat16)
        for copy in stores(i):
            copy.start()
        return carry

    lax.fori_loop(0, chunks, one_chunk, 0)
    for i in range(chunks):
        for copy in stores(i):
            copy.wait()


def on_device(fsdp, tp, momentum, gradient, basis, weight, inputs):
    rows_local, width = momentum.shape
    rank = basis.shape[0]
    rows = rows_local * fsdp
    tokens = inputs.shape[0]
    depth = fsdp // 8
    assert depth * 8 == fsdp and rank <= SUB
    scale = step_size * math.sqrt(width * tp / rows)
    block = CHUNK * LANES
    padded = -(-width // block) * block
    groups = padded // LANES
    chunks = groups // CHUNK

    def dense(array):
        if padded != width:
            array = jnp.pad(array, ((0, 0), (0, padded - width)))
        return array.reshape(array.shape[0], groups, LANES)

    as_it_lies = rows_local == 1 and padded == width
    m, g = dense(momentum), dense(gradient)
    w = weight if as_it_lies else dense(weight)
    b = dense(basis).transpose(1, 0, 2).reshape(groups * rank, LANES)
    if tp > 1:
        buffer = decay_rate * momentum + gradient
        power = lax.psum(
            lax.dot_general(buffer, basis, (((1,), (1,)), ((), ())), precision=highest,
                            preferred_element_type=jnp.float32), "tp")
        power = jnp.pad(power, ((0, 0), (0, SUB - rank))).reshape(rows_local * SUB, 1)
        power = jnp.broadcast_to(power, (rows_local * SUB, LANES))
    else:
        power = inputs.T

    vmem = pl.BlockSpec(memory_space=pltpu.VMEM)
    hbm = pl.BlockSpec(memory_space=pltpu.HBM)
    anywhere = pl.BlockSpec(memory_space=pl.ANY)
    unit = SUB * -(-groups // (SUB * fsdp))
    assert groups % unit == 0
    parts = 3 + len(split_chunks(WEIGHT_PLAN, chunks))
    f32, bf16 = jnp.float32, jnp.bfloat16
    slot = (rank * unit, LANES)
    stack = 8
    while stack > 1 and stack * rows > 2 * LANES:
        stack //= 2
    wide, w_dense, coeff, buffer, x, ortho, mine, squares = pl.pallas_call(
        functools.partial(gather_kernel, depth, rank, rows_local, unit, tp > 1),
        out_shape=(
            jax.ShapeDtypeStruct((chunks, CHUNK * rows, LANES), bf16),
            jax.ShapeDtypeStruct((rows_local, groups, LANES), bf16),
            jax.ShapeDtypeStruct((rank, groups, LANES), f32),
            jax.ShapeDtypeStruct((rows_local, groups, LANES), f32),
            jax.ShapeDtypeStruct((stack * tokens, stack * rows), bf16),
            jax.ShapeDtypeStruct((rows * SUB, LANES), f32),
            jax.ShapeDtypeStruct((rows_local * SUB, LANES), f32),
            jax.ShapeDtypeStruct((SUB, LANES), f32),
        ),
        in_specs=[hbm] * 4 + [vmem, vmem if tp > 1 else hbm],
        out_specs=(anywhere,) + (vmem,) * 7,
        scratch_shapes=[
            pltpu.VMEM((depth, 2, 2, 2, rows_local, groups, LANES), bf16),
            pltpu.VMEM((chunks, CHUNK * rows, LANES), bf16),
            pltpu.VMEM((rows * PITCH, LANES), f32),
            pltpu.VMEM(m.shape, f32),
            pltpu.VMEM(g.shape, f32),
            pltpu.VMEM(b.shape, f32),
            pltpu.VMEM((rows, tokens), bf16),
            pltpu.VMEM((depth, 2, 2, 2) + slot, f32),
            pltpu.VMEM((len(PLANE), depth) + slot, f32),
            pltpu.VMEM((depth,) + slot, f32),
            pltpu.VMEM((depth,) + slot, f32),
            pltpu.VMEM((depth, 2, 2, 2) + slot, bf16),
            pltpu.VMEM((depth, 2, 2, 2, rows_local * SUB, LANES), f32),
            pltpu.SemaphoreType.DMA((parts, len(PLANE) + depth)),
            pltpu.SemaphoreType.DMA((parts, len(PLANE) + depth)),
            pltpu.SemaphoreType.DMA((4,)),
            pltpu.SemaphoreType.DMA((parts,)),
        ],
        compiler_params=pltpu.CompilerParams(
            collective_id=0, has_side_effects=True, vmem_limit_bytes=63 * 1024 * 1024
        ),
        name="gather_rows",
    )(m, g, b, inputs.T, w, power)

    if tp > 1:
        squares = lax.psum(squares, "tp")

    act, nm, nb, nw = pl.pallas_call(
        functools.partial(apply_kernel, scale, rank, rows_local),
        out_shape=(
            jax.ShapeDtypeStruct((tokens, padded), bf16),
            jax.ShapeDtypeStruct((rows_local, groups, LANES), f32),
            jax.ShapeDtypeStruct((groups * rank, LANES), f32),
            jax.ShapeDtypeStruct((1, width) if as_it_lies else (rows_local, groups, LANES), bf16),
        ),
        in_specs=[vmem] * 4 + [anywhere] + [vmem] * 3,
        out_specs=(anywhere, vmem, vmem, vmem),
        scratch_shapes=[
            pltpu.VMEM((chunks, CHUNK * rows, LANES), bf16),
            pltpu.VMEM((chunks, tokens, block), bf16),
            pltpu.SemaphoreType.DMA((chunks,)),
            pltpu.SemaphoreType.DMA((chunks, STORES)),
        ],
        compiler_params=pltpu.CompilerParams(vmem_limit_bytes=63 * 1024 * 1024),
        name="apply_update",
    )(ortho, mine, squares, x, wide, coeff, buffer, w_dense)

    def flat(array):
        return array.reshape(array.shape[0], padded)[:, :width]

    new_basis = flat(nb.reshape(groups, rank, LANES).transpose(1, 0, 2))
    return flat(nm), new_basis, nw if as_it_lies else flat(nw), act[:, :width]


def solution(mesh):
    return jax.shard_map(
        functools.partial(on_device, mesh.shape["fsdp"], mesh.shape["tp"]),
        mesh=mesh,
        in_specs=(
            P("fsdp", "tp"),
            P("fsdp", "tp"),
            P(None, "tp"),
            P("fsdp", "tp"),
            P("fsdp", None),
        ),
        out_specs=(P("fsdp", "tp"), P(None, "tp"), P("fsdp", "tp"), P("fsdp", "tp")),
        check_vma=False,
    )
```

```python
import functools
import math

import jax
import jax.numpy as jnp
from jax import lax
from jax.experimental import pallas as pl
from jax.experimental.pallas import tpu as pltpu
from jax.sharding import PartitionSpec as P

decay_rate = 0.8
step_size = 0.5
epsilon = 1e-06
highest = lax.Precision.HIGHEST
MESH = pl.DeviceIdType.MESH
LANES = 128
PLANE = [(y, x, c) for y in range(2) for x in range(2) for c in range(2)][1:]
CHUNK = 16
STORES = 4
PITCH = 24
SUB = 8

WEIGHT_PLAN = (("yzx", 2), ("xzy", 2), ("zxy", 5), ("zyx", 4))


def split_chunks(plan, chunks):
    total = sum(share for _, share in plan)
    parts, start, seen = [], 0, 0
    for order, share in plan:
        seen += share
        stop = (chunks * seen) // total
        if stop > start:
            parts.append((order, start, stop - start))
        start = stop
    return parts


class Mover:
    def __init__(self, buf, window, order, number, coords, depth, send_sem, recv_sem):
        self.buf, self.window, self.order, self.number = buf, window, order, number
        self.coords, self.depth = coords, depth
        self.send_sem, self.recv_sem = send_sem, recv_sem
        self.sent = []
        self.phase = 0

    def block(self, **fixed):
        done = self.order[: self.phase]
        index = []
        for axis in "zyxc":
            if axis in fixed:
                index.append(fixed[axis])
            elif axis in done:
                index.append(slice(None))
            else:
                index.append(self.coords[axis])
        return self.buf.at[tuple(index) + self.window]

    def copy(self, ref, slot, **target):
        where = dict(self.coords, **target)
        device = ((where["z"] * 2 + where["y"]) * 2 + where["x"]) * 2 + where["c"]
        return pltpu.make_async_remote_copy(
            src_ref=ref,
            dst_ref=ref,
            send_sem=self.send_sem.at[self.number, slot],
            recv_sem=self.recv_sem.at[self.number, slot],
            device_id={"fsdp": device},
            device_id_type=MESH,
        )

    def hops(self):
        axis = self.order[self.phase]
        base = self.order.index(axis) if axis != "z" else 4
        if axis == "z":
            return [(4 + k, (self.coords["z"] + k) % self.depth, (self.coords["z"] + self.depth - k) % self.depth)
                    for k in range(1, self.depth)]
        other = 1 - self.coords[axis]
        return [(base if base < 2 else 2, other, other)]

    def start(self):
        axis = self.order[self.phase]
        for slot, target, _ in self.hops():
            copy = self.copy(self.block(), slot, **{axis: target})
            copy.start()
            self.sent.append(copy)

    def finish(self):
        axis = self.order[self.phase]
        for slot, _, source in self.hops():
            self.copy(self.block(**{axis: source}), slot, **{axis: source}).wait_recv()
        self.phase += 1

    def to_sibling(self, last):
        axis = self.order[2]
        side = 1 - self.coords[axis] if last else self.coords[axis]
        copy = self.copy(self.block(**{axis: side}), 3 if last else 4, c=1 - self.coords["c"])
        copy.start()
        self.sent.append(copy)

    def from_sibling(self):
        axis, other = self.order[2], 1 - self.coords["c"]
        for side, slot in ((self.coords[axis], 4), (1 - self.coords[axis], 3)):
            self.copy(self.block(**{axis: side, "c": other}), slot, c=other).wait_recv()

    def drain(self):
        for copy in self.sent:
            copy.wait_send()


def gather_kernel(depth, rank, rows_local, unit, has_power, *refs):
    (m_hbm, g_hbm, basis_hbm, xt_hbm, w_ref, power_ref, wide_hbm, w_out, coeff_ref, buffer_ref, x_ref, ortho_ref, mine_ref,
     squares_ref, gathered, wide, spread, m_ref, g_ref, basis_ref, xt_ref, sums, from_plane, z_sums, from_z, coeff_buf, power_buf,
     send_sem, recv_sem, local_sem, wide_sem) = refs
    groups = m_ref.shape[1]
    chunks = groups // CHUNK
    me = lax.axis_index("fsdp")
    coords = {"z": me // 8, "y": (me // 4) % 2, "x": (me // 2) % 2, "c": me % 2}
    here = (coords["z"], coords["y"], coords["x"], coords["c"])

    def number(z, y, x, c):
        return ((z * 2 + y) * 2 + x) * 2 + c

    z, y, x, c = here
    peers = [((y + dy) % 2, (x + dx) % 2, (c + dc) % 2) for dy, dx, dc in PLANE]
    partners = [number((z + k) % depth, y, x, c) for k in range(1, depth)]
    partners += [number(z, *peer) for peer in peers]
    barrier = pltpu.get_barrier_semaphore()
    for partner in partners:
        pl.semaphore_signal(barrier, inc=1, device_id={"fsdp": partner}, device_id_type=MESH)

    loads = [
        pltpu.make_async_copy(source, target, local_sem.at[i])
        for i, (source, target) in enumerate(
            ((m_hbm, m_ref), (g_hbm, g_ref), (basis_hbm, basis_ref), (xt_hbm, xt_ref))
        )
    ]
    for load in loads:
        load.start()
    if len(w_ref.shape) == 3:
        w_out[...] = w_ref[...]
    else:
        for first in range(0, groups, CHUNK):
            lines = [w_ref[:, pl.ds((first + j) * LANES, LANES)].astype(jnp.float32) for j in range(CHUNK)]
            w_out[0, pl.ds(first, CHUNK)] = jnp.concatenate(lines, axis=0).astype(jnp.bfloat16)
    gathered[here] = w_out[...]

    def mover(buf, window, order, count):
        return Mover(buf, window, order, count, coords, depth, send_sem, recv_sem)

    late = []
    pieces = split_chunks(WEIGHT_PLAN, chunks)
    for order, start, count in pieces:
        window = (slice(None), pl.ds(start * CHUNK, count * CHUNK), slice(None))
        late.append(mover(gathered, window, order, 3 + len(late)))

    pl.semaphore_wait(barrier, len(partners))
    for part in late:
        part.start()
    for load in loads[:3]:
        load.wait()

    for row in range(rows_local):
        buffer_ref[row] = decay_rate * m_ref[row] + g_ref[row]
        if has_power:
            power_buf[here + (pl.ds(row * SUB, SUB),)] = power_ref[pl.ds(row * SUB, SUB)]
        else:
            tile = [
                jnp.broadcast_to(
                    jnp.sum(buffer_ref[row] * basis_ref[pl.ds(k, groups, stride=rank)], keepdims=True), (1, LANES)
                )
                for k in range(rank)
            ]
            tile += [jnp.zeros((1, LANES), jnp.float32)] * (SUB - rank)
            power_buf[here + (pl.ds(row * SUB, SUB),)] = jnp.concatenate(tile, axis=0)

    devices = [(z, y, x, c) for z in range(depth) for y in range(2) for x in range(2) for c in range(2)]
    owners = groups // unit
    own_power = [power_buf[here + (pl.ds(row * SUB, SUB),)] for row in range(rows_local)]
    for i, d in enumerate(devices):
        if i >= owners:
            sums[d] = jnp.zeros((rank * unit, LANES), jnp.float32)
            continue
        terms = []
        for k in range(rank):
            term = jnp.zeros((unit, LANES), jnp.float32)
            for row in range(rows_local):
                term = term + own_power[row][k : k + 1] * buffer_ref[row, pl.ds(i * unit, unit)]
            terms.append(term)
        sums[d] = jnp.concatenate(terms, axis=0)

    def advance(movers):
        for part in movers:
            part.finish()
            if part.phase == 2:
                part.to_sibling(False)
            if part.phase < 3:
                part.start()
            else:
                part.to_sibling(True)

    def move(source, target, number_of, slot, device):
        return pltpu.make_async_remote_copy(
            src_ref=source, dst_ref=target, send_sem=send_sem.at[number_of, slot],
            recv_sem=recv_sem.at[number_of, slot], device_id={"fsdp": device}, device_id_type=MESH,
        )

    column = (slice(None), y, x, c)
    hops_z = [((z + k) % depth, (z + depth - k) % depth) for k in range(1, depth)]
    small = []

    def begin(copies):
        for copy in copies:
            copy.start()
        small.extend(copies)

    def spread_z(buf, number_of):
        begin([move(buf.at[here], buf.at[here], number_of, len(PLANE) + k, number(there, y, x, c))
               for k, (there, _) in enumerate(hops_z)])

    def spread_plane(buf, number_of):
        for k, (_, source) in enumerate(hops_z):
            slot = buf.at[source, y, x, c]
            move(slot, slot, number_of, len(PLANE) + k, number(source, y, x, c)).wait_recv()
        begin([move(buf.at[column], buf.at[column], number_of, k, number(z, *peer)) for k, peer in enumerate(peers)])

    def arrived(buf, number_of):
        for k, peer in enumerate(peers):
            slot = buf.at[(slice(None),) + peer]
            move(slot, slot, number_of, k, number(z, *peer)).wait_recv()

    first, last = late[:2], late[2:]
    spread_z(power_buf, 0)
    to_plane = [move(sums.at[(slice(None),) + peer], from_plane.at[k], 2, k, number(z, *peer))
                for k, peer in enumerate(peers)]
    begin(to_plane)
    advance(first)
    spread_plane(power_buf, 0)
    loads[3].wait()
    tokens = xt_ref.shape[1]
    features = jnp.transpose(xt_ref[...].astype(jnp.float32)).astype(jnp.bfloat16)
    for b in range(x_ref.shape[0] // tokens):
        shape = (xt_ref.shape[0], x_ref.shape[1])
        place = lax.broadcasted_iota(jnp.int32, shape, 1) == (
            lax.broadcasted_iota(jnp.int32, shape, 0) + b * shape[0]
        )
        x_ref[pl.ds(b * tokens, tokens)] = jnp.dot(
            features, jnp.where(place, 1.0, 0.0).astype(jnp.bfloat16), preferred_element_type=jnp.float32
        ).astype(jnp.bfloat16)
    for copy in to_plane:
        copy.wait_recv()
    for i in range(depth):
        total = sums[i, y, x, c]
        for k in range(len(PLANE)):
            total = total + from_plane[k, i]
        z_sums[i] = total
    over_z = [move(z_sums.at[there], from_z.at[k], 2, len(PLANE) + k, number(there, y, x, c))
              for k, (there, _) in enumerate(hops_z)]
    begin(over_z)
    advance(last)
    arrived(power_buf, 0)

    tiles = [power_buf[d + (pl.ds(row * SUB, SUB),)] for d in devices for row in range(rows_local)]
    gram = []
    for l in range(rank):
        total = jnp.zeros((SUB, LANES), jnp.float32)
        for tile in tiles:
            total = total + tile * tile[l : l + 1]
        gram.append(total)
    lower = [[None] * rank for _ in range(rank)]
    inverse = [None] * rank
    for l in range(rank):
        value = gram[l][l : l + 1]
        for j in range(l):
            value = value - lower[l][j] * lower[l][j]
        lower[l][l] = jnp.sqrt(value)
        inverse[l] = 1.0 / lower[l][l]
        for k in range(l + 1, rank):
            value = gram[l][k : k + 1]
            for j in range(l):
                value = value - lower[k][j] * lower[l][j]
            lower[k][l] = value * inverse[l]

    def solve(right):
        found = []
        for k in range(rank):
            value = right[k]
            for j in range(k):
                value = value - lower[k][j] * found[j]
            found.append(value * inverse[k])
        return found

    for copy in over_z:
        copy.wait_recv()
    total = z_sums[z]
    for k in range(depth - 1):
        total = total + from_z[k]
    coeff_buf[here] = jnp.concatenate(
        solve([total[k * unit : (k + 1) * unit] for k in range(rank)]), axis=0
    ).astype(jnp.bfloat16)
    spread_z(coeff_buf, 1)
    advance(last)

    filler = [jnp.zeros((1, LANES), jnp.float32)] * (SUB - rank)
    for i, tile in enumerate(tiles):
        found = solve([tile[k : k + 1] for k in range(rank)])
        ortho_ref[pl.ds(i * SUB, SUB)] = jnp.concatenate(found + filler, axis=0)
    for row in range(rows_local):
        tile = own_power[row]
        found = solve([tile[k : k + 1] for k in range(rank)])
        mine_ref[pl.ds(row * SUB, SUB)] = jnp.concatenate(found + filler, axis=0)

    spread_plane(coeff_buf, 1)
    advance(first)
    arrived(coeff_buf, 1)
    squares = [jnp.zeros((unit, LANES), jnp.float32) for _ in range(rank)]
    for i in range(owners):
        slot = coeff_buf[devices[i]].astype(jnp.float32)
        for k in range(rank):
            values = slot[k * unit : (k + 1) * unit]
            coeff_ref[k, pl.ds(i * unit, unit)] = values
            squares[k] = squares[k] + values * values
    squares_ref[...] = jnp.concatenate(
        [jnp.broadcast_to(jnp.sum(squares[k], keepdims=True), (1, LANES)) for k in range(rank)] + filler, axis=0
    )

    advance(last)

    rows = len(devices) * rows_local

    def relay(number):
        part, (_, start, count) = late[number], pieces[number]
        part.from_sibling()

        def one_chunk(i, carry):
            at = pl.ds(pl.multiple_of(i * CHUNK, CHUNK), CHUNK)
            for place, d in enumerate(devices):
                for row in range(rows_local):
                    spread[pl.ds((place * rows_local + row) * PITCH, CHUNK)] = gathered[d + (row, at)].astype(
                        jnp.float32
                    )
            for j in range(CHUNK):
                wide[i, pl.ds(j * rows, rows)] = spread[pl.ds(j, rows, stride=PITCH)].astype(jnp.bfloat16)
            return carry

        lax.fori_loop(start, start + count, one_chunk, 0)
        copy = pltpu.make_async_copy(
            wide.at[pl.ds(start, count)], wide_hbm.at[pl.ds(start, count)], wide_sem.at[number]
        )
        copy.start()
        return copy

    copies = []
    if len(late) <= 2:
        advance(first)
    for number in range(2, len(late)):
        copies.append(relay(number))
        if number == 2:
            advance(first)
    for number in range(min(2, len(late))):
        copies.append(relay(number))
    for copy in copies:
        copy.wait()
    for part in late:
        part.drain()
    for copy in small:
        copy.wait_send()


def apply_kernel(scale, rank, rows_local, ortho_ref, mine_ref, squares_ref, x_ref, wide_hbm, coeff_ref, buffer_ref,
                 w_ref, act_hbm, nm_ref, nb_ref, nw_ref, wide, act_ref, load_sem, store_sem):
    chunks = wide_hbm.shape[0]
    rows = wide_hbm.shape[1] // CHUNK
    block = CHUNK * LANES
    ortho = [ortho_ref[pl.ds(k, rows, stride=SUB)] for k in range(rank)]
    inverse = [1.0 / jnp.sqrt(squares_ref[k : k + 1] + epsilon) for k in range(rank)]

    def load(i):
        return pltpu.make_async_copy(wide_hbm.at[i], wide.at[i], load_sem.at[i])

    share = act_ref.shape[1] // STORES

    def stores(i):
        at = pl.ds(pl.multiple_of(i * block, block), block)
        return [
            pltpu.make_async_copy(
                act_ref.at[i, pl.ds(q * share, share)], act_hbm.at[pl.ds(q * share, share), at], store_sem.at[i, q]
            )
            for q in range(STORES)
        ]

    for i in range(chunks):
        load(i).start()

    def one_chunk(i, carry):
        at = pl.ds(pl.multiple_of(i * CHUNK, CHUNK), CHUNK)
        coeff = [coeff_ref[k, at] for k in range(rank)]
        basis = [coeff[k] * inverse[k] for k in range(rank)]
        for k in range(rank):
            nb_ref[pl.ds(i * (CHUNK * rank) + k, CHUNK, stride=rank)] = basis[k]
        scaled = [scale * basis[k] for k in range(rank)]

        def lowered(weight, ref, row):
            change = ref[pl.ds(row * SUB, 1)] * scaled[0]
            for k in range(1, rank):
                change = change + ref[pl.ds(row * SUB + k, 1)] * scaled[k]
            return weight.astype(jnp.float32) - change

        for row in range(rows_local):
            lowered_row = lowered(w_ref[row, at], mine_ref, row)
            if len(nw_ref.shape) == 3:
                nw_ref[row, at] = lowered_row.astype(jnp.bfloat16)
            else:
                line = jnp.concatenate([lowered_row[j : j + 1] for j in range(CHUNK)], axis=1)
                nw_ref[:, pl.ds(pl.multiple_of(i * block, block), block)] = line.astype(jnp.bfloat16)
            feedback = mine_ref[pl.ds(row * SUB, 1)] * coeff[0]
            for k in range(1, rank):
                feedback = feedback + mine_ref[pl.ds(row * SUB + k, 1)] * coeff[k]
            nm_ref[row, at] = buffer_ref[row, at] - (1.0 - decay_rate) * feedback
        load(i).wait()
        tiles = []
        for j in range(CHUNK):
            change = ortho[0] * scaled[0][j : j + 1]
            for k in range(1, rank):
                change = change + ortho[k] * scaled[k][j : j + 1]
            tile = wide[i, pl.ds(j * rows, rows)].astype(jnp.float32) - change
            tiles.append(tile.astype(jnp.bfloat16))

        tokens = act_ref.shape[1]
        stack = x_ref.shape[0] // tokens
        pairs = [jnp.concatenate(tiles[j : j + 2], axis=1) for j in range(0, CHUNK, 2)]
        for first in range(0, len(pairs), stack):
            weights = jnp.concatenate(pairs[first : first + stack], axis=0)
            for b in range(stack):
                act_ref[i, :, pl.ds((first + b) * 2 * LANES, 2 * LANES)] = jnp.dot(
                    x_ref[pl.ds(b * tokens, tokens)], weights, preferred_element_type=jnp.float32
                ).astype(jnp.bfloat16)
        for copy in stores(i):
            copy.start()
        return carry

    lax.fori_loop(0, chunks, one_chunk, 0)
    for i in range(chunks):
        for copy in stores(i):
            copy.wait()


def on_device(fsdp, tp, momentum, gradient, basis, weight, inputs):
    rows_local, width = momentum.shape
    rank = basis.shape[0]
    rows = rows_local * fsdp
    tokens = inputs.shape[0]
    depth = fsdp // 8
    assert depth * 8 == fsdp and rank <= SUB
    scale = step_size * math.sqrt(width * tp / rows)
    block = CHUNK * LANES
    padded = -(-width // block) * block
    groups = padded // LANES
    chunks = groups // CHUNK

    def dense(array):
        if padded != width:
            array = jnp.pad(array, ((0, 0), (0, padded - width)))
        return array.reshape(array.shape[0], groups, LANES)

    as_it_lies = rows_local == 1 and padded == width
    m, g = dense(momentum), dense(gradient)
    w = weight if as_it_lies else dense(weight)
    b = dense(basis).transpose(1, 0, 2).reshape(groups * rank, LANES)
    if tp > 1:
        buffer = decay_rate * momentum + gradient
        power = lax.psum(
            lax.dot_general(buffer, basis, (((1,), (1,)), ((), ())), precision=highest,
                            preferred_element_type=jnp.float32), "tp")
        power = jnp.pad(power, ((0, 0), (0, SUB - rank))).reshape(rows_local * SUB, 1)
        power = jnp.broadcast_to(power, (rows_local * SUB, LANES))
    else:
        power = inputs.T

    vmem = pl.BlockSpec(memory_space=pltpu.VMEM)
    hbm = pl.BlockSpec(memory_space=pltpu.HBM)
    anywhere = pl.BlockSpec(memory_space=pl.ANY)
    unit = SUB * -(-groups // (SUB * fsdp))
    assert groups % unit == 0
    parts = 3 + len(split_chunks(WEIGHT_PLAN, chunks))
    f32, bf16 = jnp.float32, jnp.bfloat16
    slot = (rank * unit, LANES)
    stack = 8
    while stack > 1 and stack * rows > 2 * LANES:
        stack //= 2
    wide, w_dense, coeff, buffer, x, ortho, mine, squares = pl.pallas_call(
        functools.partial(gather_kernel, depth, rank, rows_local, unit, tp > 1),
        out_shape=(
            jax.ShapeDtypeStruct((chunks, CHUNK * rows, LANES), bf16),
            jax.ShapeDtypeStruct((rows_local, groups, LANES), bf16),
            jax.ShapeDtypeStruct((rank, groups, LANES), f32),
            jax.ShapeDtypeStruct((rows_local, groups, LANES), f32),
            jax.ShapeDtypeStruct((stack * tokens, stack * rows), bf16),
            jax.ShapeDtypeStruct((rows * SUB, LANES), f32),
            jax.ShapeDtypeStruct((rows_local * SUB, LANES), f32),
            jax.ShapeDtypeStruct((SUB, LANES), f32),
        ),
        in_specs=[hbm] * 4 + [vmem, vmem if tp > 1 else hbm],
        out_specs=(anywhere,) + (vmem,) * 7,
        scratch_shapes=[
            pltpu.VMEM((depth, 2, 2, 2, rows_local, groups, LANES), bf16),
            pltpu.VMEM((chunks, CHUNK * rows, LANES), bf16),
            pltpu.VMEM((rows * PITCH, LANES), f32),
            pltpu.VMEM(m.shape, f32),
            pltpu.VMEM(g.shape, f32),
            pltpu.VMEM(b.shape, f32),
            pltpu.VMEM((rows, tokens), bf16),
            pltpu.VMEM((depth, 2, 2, 2) + slot, f32),
            pltpu.VMEM((len(PLANE), depth) + slot, f32),
            pltpu.VMEM((depth,) + slot, f32),
            pltpu.VMEM((depth,) + slot, f32),
            pltpu.VMEM((depth, 2, 2, 2) + slot, bf16),
            pltpu.VMEM((depth, 2, 2, 2, rows_local * SUB, LANES), f32),
            pltpu.SemaphoreType.DMA((parts, len(PLANE) + depth)),
            pltpu.SemaphoreType.DMA((parts, len(PLANE) + depth)),
            pltpu.SemaphoreType.DMA((4,)),
            pltpu.SemaphoreType.DMA((parts,)),
        ],
        compiler_params=pltpu.CompilerParams(
            collective_id=0, has_side_effects=True, vmem_limit_bytes=63 * 1024 * 1024
        ),
        name="gather_rows",
    )(m, g, b, inputs.T, w, power)

    if tp > 1:
        squares = lax.psum(squares, "tp")

    act, nm, nb, nw = pl.pallas_call(
        functools.partial(apply_kernel, scale, rank, rows_local),
        out_shape=(
            jax.ShapeDtypeStruct((tokens, padded), bf16),
            jax.ShapeDtypeStruct((rows_local, groups, LANES), f32),
            jax.ShapeDtypeStruct((groups * rank, LANES), f32),
            jax.ShapeDtypeStruct((1, width) if as_it_lies else (rows_local, groups, LANES), bf16),
        ),
        in_specs=[vmem] * 4 + [anywhere] + [vmem] * 3,
        out_specs=(anywhere, vmem, vmem, vmem),
        scratch_shapes=[
            pltpu.VMEM((chunks, CHUNK * rows, LANES), bf16),
            pltpu.VMEM((chunks, tokens, block), bf16),
            pltpu.SemaphoreType.DMA((chunks,)),
            pltpu.SemaphoreType.DMA((chunks, STORES)),
        ],
        compiler_params=pltpu.CompilerParams(vmem_limit_bytes=63 * 1024 * 1024),
        name="apply_update",
    )(ortho, mine, squares, x, wide, coeff, buffer, w_dense)

    def flat(array):
        return array.reshape(array.shape[0], padded)[:, :width]

    new_basis = flat(nb.reshape(groups, rank, LANES).transpose(1, 0, 2))
    return flat(nm), new_basis, nw if as_it_lies else flat(nw), act[:, :width]


def solution(mesh):
    return jax.shard_map(
        functools.partial(on_device, mesh.shape["fsdp"], mesh.shape["tp"]),
        mesh=mesh,
        in_specs=(
            P("fsdp", "tp"),
            P("fsdp", "tp"),
            P(None, "tp"),
            P("fsdp", "tp"),
            P("fsdp", None),
        ),
        out_specs=(P("fsdp", "tp"), P(None, "tp"), P("fsdp", "tp"), P("fsdp", "tp")),
        check_vma=False,
    )
```
